512 devices in a mesh: sn: 64 (over x, z), rhs: 8 (over y, core).
Axes of the slice: x: 4, y: 4, z: 16, core: 2. Of those that a mesh axis runs over, the one named last changes fastest.
Arguments:
- lanczos_block: float32 [512, 8, 16384], P(None, None, ('sn', 'rhs')), may hold values from -6 to 6
- diag_inv: bfloat16 [8, 128, 128, 128], P(None, 'sn')
- factor_tiles: bfloat16 [7, 1536, 128, 128], P(None, 'sn'), may hold values from -0.046875 to 0.046875
- tile_rows: int32 [7, 1536], replicated, may hold values from 128 to 1023, as said below
- tile_cols: int32 [7, 1536], replicated, may hold values from 0 to 895, as said below
Outputs:
- solution: bfloat16 [512, 8, 16384], P(None, None, ('sn', 'rhs'))
The draws below stay inside these ranges and needn't reach their ends.
Inputs may be any that keep to these rules, and one draw needn't show every extreme that they name: Slot j of level l belongs to device j // 24; tile_rows[l, j] is a supernode of a level above l whose position lies among that device's positions, 2 * (j // 24) to 2 * (j // 24) + 1. tile_cols[l, j] is a supernode of level l whose position belongs to device (j // 24 + (j % 24) // 8 - 1) modulo 64, that is, positions 2 times that device to 2 times that device + 1.
All inputs are finite; a program needn't handle non-finite values.
Results may differ from the reference program's by a relative error of at most 0.011.
Values may be sent and summed in bfloat16 or wider, within the bound.
No kernel may reach another device: no remote copies, remote signals or barrier semaphores. Data moves between devices by JAX's collectives and lax.ppermute only.
A program may use at most 64 MiB of HBM per device.

```python
import jax
import jax.numpy as jnp
from jax import lax

B = 128
NRHS = 512
LEVELS = 8
LVL_DEV = 2
TPG = 8
PER_LEVEL = 128
N_SN = 64


def tile_pattern(key):
    grid_shape = (LEVELS - 1, N_SN * 3 * TPG)
    col_level = jnp.arange(LEVELS - 1, dtype=jnp.int32)[:, None]
    slot_index = jnp.arange(N_SN * 3 * TPG, dtype=jnp.int32)[None, :]
    holder = slot_index // (3 * TPG)
    offset = slot_index % (3 * TPG) // TPG - 1
    first_key = jax.random.fold_in(key, 101)
    second_key = jax.random.fold_in(key, 202)
    third_key = jax.random.fold_in(key, 303)
    row_level = col_level + 1 + jax.random.randint(first_key, grid_shape, 0, LEVELS - 1 - col_level, dtype=jnp.int32)
    row_pick = jax.random.randint(second_key, grid_shape, 0, LVL_DEV, dtype=jnp.int32)
    col_pick = jax.random.randint(third_key, grid_shape, 0, LVL_DEV, dtype=jnp.int32)
    rows_out = row_level * PER_LEVEL + holder * LVL_DEV + row_pick
    cols_out = col_level * PER_LEVEL + (holder + offset) % N_SN * LVL_DEV + col_pick
    return (rows_out.astype(jnp.int32), cols_out.astype(jnp.int32))


def draw_tile_rows(key, part):
    return tile_pattern(key)[0]


def draw_tile_cols(key, part):
    return tile_pattern(key)[1]


def draw_diag_inv(key, part):
    grid_shape = (LEVELS, PER_LEVEL, B, B)
    base_key = jax.random.fold_in(key, 7)
    off_key, diag_key = jax.random.split(base_key)
    row_ids = jnp.arange(B)[:, None]
    col_ids = jnp.arange(B)[None, :]
    spread = 0.12 * jax.random.normal(off_key, grid_shape, jnp.float32)
    middle = jax.random.uniform(diag_key, grid_shape, jnp.float32, 0.6, 1.4)
    below = jnp.where(row_ids > col_ids, spread, 0.0)
    return (below + jnp.where(row_ids == col_ids, middle, 0.0)).astype(jnp.bfloat16)


def block_scale(own_key, shape, cuts, low, largest):
    gain = 1.0
    for axis_at, shards_of in cuts:
        draws = jax.random.uniform(jax.random.fold_in(jax.random.fold_in(own_key, 6), axis_at), (shards_of,), jnp.float32, low / len(cuts), largest / len(cuts))
        gain = gain * jnp.repeat(jnp.exp(draws), shape[axis_at] // shards_of).reshape((-1,) + (1,) * (len(shape) - 1 - axis_at))
    return gain


def centred(key, extent, scale, most, cuts=(), held_as=jnp.bfloat16):
    level = block_scale(key, extent, cuts, -0.22, 0.18) if cuts else 1.0
    values = jax.random.normal(key, extent, jnp.float32) * scale * level
    return jnp.minimum(jnp.maximum(values, -most), most).astype(held_as)


def setup_inputs(seed: int = 0) -> dict:
    seeds = jax.random.split(jax.random.key(seed), 6)
    lanczos_block = centred(seeds[0], (NRHS, LEVELS, PER_LEVEL * B), 1.0, 6.0, ((2, 512),), jnp.float32)
    diag_inv = draw_diag_inv(jax.random.fold_in(seeds[5], 71), 0)
    factor_tiles = centred(seeds[2], (LEVELS - 1, N_SN * 3 * TPG, B, B), (32 * B * TPG // LVL_DEV) ** -0.5, 0.046875, ((1, 64),))
    tile_rows = draw_tile_rows(jax.random.fold_in(seeds[5], 71), 0)
    tile_cols = draw_tile_cols(jax.random.fold_in(seeds[5], 71), 0)
    return dict(lanczos_block=lanczos_block, diag_inv=diag_inv, factor_tiles=factor_tiles, tile_rows=tile_rows, tile_cols=tile_cols)


def reference(lanczos_block, diag_inv, factor_tiles, tile_rows, tile_cols):
    columns = lanczos_block.shape[0]
    vectors = lanczos_block.reshape(columns, LEVELS * PER_LEVEL, B)
    updates = jnp.zeros((columns, LEVELS * PER_LEVEL, B), jnp.float32)
    solved = []
    for height in range(LEVELS):
        start_slot = height * PER_LEVEL
        reduced = (vectors[:, start_slot:start_slot + PER_LEVEL] - updates[:, start_slot:start_slot + PER_LEVEL]).astype(jnp.bfloat16)
        solved_now = jnp.einsum('rqb,qab->rqa', reduced.astype(jnp.float32), diag_inv[height].astype(jnp.float32), precision=lax.Precision.HIGHEST).astype(jnp.bfloat16)
        solved.append(solved_now)
        if height + 1 < LEVELS:
            picked = solved_now[:, (tile_cols[height] - start_slot).astype(jnp.int32)]
            partial_value = jnp.einsum('rtb,tab->rta', picked.astype(jnp.float32), factor_tiles[height].astype(jnp.float32), precision=lax.Precision.HIGHEST)
            updates = updates.at[:, tile_rows[height].astype(jnp.int32)].add(partial_value)
    answers = jnp.zeros((columns, LEVELS * PER_LEVEL, B), jnp.bfloat16)
    for height in reversed(range(LEVELS)):
        start_slot = height * PER_LEVEL
        if height + 1 < LEVELS:
            picked = answers[:, tile_rows[height].astype(jnp.int32)]
            partial_value = jnp.einsum('rta,tab->rtb', picked.astype(jnp.float32), factor_tiles[height].astype(jnp.float32), precision=lax.Precision.HIGHEST)
            terms = jnp.zeros((columns, PER_LEVEL, B), jnp.float32).at[:, (tile_cols[height] - start_slot).astype(jnp.int32)].add(partial_value)
            reduced = (solved[height].astype(jnp.float32) - terms).astype(jnp.bfloat16)
        else:
            reduced = solved[height]
        answer = jnp.einsum('rqa,qab->rqb', reduced.astype(jnp.float32), diag_inv[height].astype(jnp.float32), precision=lax.Precision.HIGHEST).astype(jnp.bfloat16)
        answers = answers.at[:, start_slot:start_slot + PER_LEVEL].set(answer)
    return answers.reshape(columns, LEVELS, PER_LEVEL * B)
```

```python
import jax
import jax.numpy as jnp
from jax import lax
from jax.experimental import pallas as pl
from jax.experimental.pallas import tpu as pltpu
from jax.sharding import PartitionSpec as P

BF = jnp.bfloat16
F32 = jnp.float32


def build_operators(tiles, diag, row_slot, col_slot):
    levels, owned, b, _ = diag.shape
    count = tiles.shape[1]
    wide = 3 * owned * b
    tall = owned * b

    def body(row_ref, col_ref, t_ref, d_ref, *outs):
        s_refs, b_refs = outs[: levels - 1], outs[levels - 1 :]
        for l in range(levels - 1):
            s_refs[l][...] = jnp.zeros_like(s_refs[l])

            def add(t, carry):
                r = pl.multiple_of(row_ref[l, t] * b, b)
                c = pl.multiple_of(col_ref[l, t] * b, b)
                at = (pl.ds(r, b), pl.ds(c, b))
                s_refs[l][at] = s_refs[l][at] + t_ref[l, t]
                return carry

            lax.fori_loop(0, count, add, 0, unroll=4)
            for q in range(owned):
                rows = slice(q * b, (q + 1) * b)
                b_refs[l][rows, :] = jnp.dot(
                    d_ref[l + 1, q], s_refs[l][rows, :], preferred_element_type=F32
                ).astype(BF)

    shapes = [jax.ShapeDtypeStruct(((levels - 1 - l) * tall, wide), BF) for l in range(levels - 1)]
    shapes += [jax.ShapeDtypeStruct((tall, wide), BF) for _ in range(levels - 1)]
    vmem = pl.BlockSpec(memory_space=pltpu.VMEM)
    smem = pl.BlockSpec(memory_space=pltpu.SMEM)
    outs = pl.pallas_call(
        body,
        out_shape=shapes,
        in_specs=[smem, smem, vmem, vmem],
        out_specs=[vmem] * len(shapes),
        compiler_params=pltpu.CompilerParams(vmem_limit_bytes=40 * 2**20),
        cost_estimate=pl.CostEstimate(flops=4 * 10**8, bytes_accessed=24 * 2**20, transcendentals=0),
    )(row_slot, col_slot, tiles, diag)
    return outs[: levels - 1], outs[levels - 1 :]


def dot_t(a, w):
    return lax.dot_general(a, w, (((1,), (1,)), ((), ())), preferred_element_type=F32)


def dot_n(a, w):
    return lax.dot_general(a, w, (((1,), (0,)), ((), ())), preferred_element_type=F32)


def on_device(lanczos_block, diag_inv, factor_tiles, tile_rows, tile_cols):
    levels, owned, b = diag_inv.shape[:3]
    group_tiles = factor_tiles.shape[1]
    n = lax.axis_size("sn")
    own = lax.axis_index("sn")
    per_level = owned * n
    wide = owned * b
    odd = own % 2 == 1

    panels = lax.all_to_all(lanczos_block.astype(BF), "rhs", split_axis=0, concat_axis=2, tiled=True)
    columns = panels.shape[0]

    my_rows = lax.dynamic_slice_in_dim(tile_rows, own * group_tiles, group_tiles, 1)
    my_cols = lax.dynamic_slice_in_dim(tile_cols, own * group_tiles, group_tiles, 1)
    above = jnp.arange(1, levels, dtype=jnp.int32)[:, None]
    group = (jnp.arange(group_tiles, dtype=jnp.int32) // (group_tiles // 3))[None, :]
    row_slot = (my_rows // per_level - above) * owned + my_rows % owned
    col_slot = group * owned + my_cols % owned
    S, B = build_operators(factor_tiles, diag_inv, row_slot, col_slot)

    even_pairs = [[i, i + 1] for i in range(0, n, 2)]
    odd_swap = [(i, (i + 1) % n if i % 2 else (i - 1) % n) for i in range(n)]

    def diag_fwd(l, f):
        f = f.astype(BF).reshape(columns, owned, b)
        return jnp.einsum("rkb,kab->rka", f, diag_inv[l], preferred_element_type=F32).reshape(columns, wide)

    def diag_bwd(l, e):
        e = e.reshape(columns, owned, b)
        z = jnp.einsum("rka,kab->rkb", e, diag_inv[l], preferred_element_type=F32)
        return z.astype(BF).reshape(columns, wide)

    x = [panels[:, l, :].astype(F32) for l in range(levels)]
    y = [None] * levels
    y[0] = diag_fwd(0, x[0]).astype(BF)
    for l in range(levels - 1):
        far = lax.ppermute(y[l], "sn", odd_swap)
        near = lax.all_gather(y[l], "sn", axis_index_groups=even_pairs)
        y3 = jnp.concatenate(
            [jnp.where(odd, near[0], far), y[l], jnp.where(odd, far, near[1])], axis=1
        )
        y[l + 1] = (diag_fwd(l + 1, x[l + 1]) - dot_t(y3, B[l])).astype(BF)
        if l + 2 < levels:
            older = dot_t(y3, S[l][wide:])
            for k in range(l + 2, levels):
                x[k] = x[k] - older[:, (k - l - 2) * wide : (k - l - 1) * wide]

    z = [None] * levels
    e = y[levels - 1]
    z[levels - 1] = diag_bwd(levels - 1, e)
    for l in reversed(range(levels - 1)):
        part = dot_n(e, B[l])
        if l + 2 < levels:
            part = part + dot_n(jnp.concatenate(z[l + 2 :], axis=1), S[l][wide:])
        left, mid, right = (part[:, k * wide : (k + 1) * wide] for k in range(3))
        far = lax.ppermute(jnp.where(odd, right, left).astype(BF), "sn", odd_swap)
        near = lax.all_gather(jnp.where(odd, left, right).astype(BF), "sn", axis_index_groups=even_pairs)
        terms = mid + far.astype(F32) + jnp.where(odd, near[0], near[1]).astype(F32)
        e = (y[l].astype(F32) - terms).astype(BF)
        z[l] = diag_bwd(l, e)
    combined = jnp.stack(z, axis=1)
    return lax.all_to_all(combined, "rhs", split_axis=2, concat_axis=0, tiled=True)


def solution(mesh):
    placed = (
        P(None, None, ("sn", "rhs")),
        P(None, "sn", None, None),
        P(None, "sn", None, None),
        P(),
        P(),
    )
    return jax.shard_map(
        on_device,
        mesh=mesh,
        in_specs=placed,
        out_specs=P(None, None, ("sn", "rhs")),
        check_vma=False,
    )
```

```python
import jax
import jax.numpy as jnp
from jax import lax
from jax.experimental import pallas as pl
from jax.experimental.pallas import tpu as pltpu
from jax.sharding import PartitionSpec as P

BF = jnp.bfloat16
F32 = jnp.float32
VMEM = pl.BlockSpec(memory_space=pltpu.VMEM)
SMEM = pl.BlockSpec(memory_space=pltpu.SMEM)


def dot_t(a, w):
    return lax.dot_general(a, w, (((1,), (1,)), ((), ())), preferred_element_type=F32)


def dot_n(a, w):
    return lax.dot_general(a, w, (((1,), (0,)), ((), ())), preferred_element_type=F32)


def call(body, outs, args, scratch=(), flops=10**8, mib=16):
    specs = [SMEM if a.dtype == jnp.int32 else VMEM for a in args]
    size = sum(a.size * a.dtype.itemsize for a in args)
    return pl.pallas_call(
        body,
        out_shape=[jax.ShapeDtypeStruct(s, d) for s, d in outs],
        in_specs=specs,
        out_specs=[VMEM] * len(outs),
        scratch_shapes=list(scratch),
        compiler_params=pltpu.CompilerParams(vmem_limit_bytes=mib * 2**20),
        cost_estimate=pl.CostEstimate(flops=flops, bytes_accessed=size, transcendentals=0),
    )(*args)


def build_operators(tiles, diag, row_slot, col_slot):
    levels, owned, b, _ = diag.shape
    count = tiles.shape[1]
    wide = 3 * owned * b
    tall = owned * b
    slots = [(0, 0), (1, 0), (2, 0), (3, 0), (2, 1), (3, 1), (2, 2)]

    def body(row_ref, col_ref, t_ref, d_ref, *outs):
        s_refs, b_refs = outs[: levels - 1], outs[levels - 1 :]
        for l in range(levels - 1):
            s_refs[l][...] = jnp.zeros_like(s_refs[l])

            def add(t, carry):
                r = pl.multiple_of(row_ref[l, t] * b, b)
                c = pl.multiple_of(col_ref[l, t] * b, b)
                at = (pl.ds(r, b), pl.ds(c, b))
                s_refs[l][at] = s_refs[l][at] + t_ref[l, t]
                return carry

            lax.fori_loop(0, count, add, 0, unroll=8)
            which, index = slots[l]
            for q in range(owned):
                rows = slice(q * b, (q + 1) * b)
                b_refs[which][index, rows, :] = dot_n(d_ref[l + 1, q], s_refs[l][rows, :]).astype(BF)

    outs = [(((levels - 1 - l) * tall, wide), BF) for l in range(levels - 1)]
    outs += [((k, tall, wide), BF) for k in (1, 1, 3, 2)]
    res = call(body, outs, (row_slot, col_slot, tiles, diag), flops=4 * 10**8, mib=32)
    return res[: levels - 1], res[levels - 1 :], slots


def on_device(lanczos_block, diag_inv, factor_tiles, tile_rows, tile_cols):
    levels, owned, b = diag_inv.shape[:3]
    group_tiles = factor_tiles.shape[1]
    n = lax.axis_size("sn")
    own = lax.axis_index("sn")
    per_level = owned * n
    w = owned * b
    parity = (own % 2).astype(jnp.int32).reshape(1)

    panels = lax.all_to_all(lanczos_block.astype(BF), "rhs", split_axis=0, concat_axis=2, tiled=True)
    cols = panels.shape[0]
    panels = panels.reshape(cols, levels * w)

    my_rows = lax.dynamic_slice_in_dim(tile_rows, own * group_tiles, group_tiles, 1)
    my_cols = lax.dynamic_slice_in_dim(tile_cols, own * group_tiles, group_tiles, 1)
    above = jnp.arange(1, levels, dtype=jnp.int32)[:, None]
    group = (jnp.arange(group_tiles, dtype=jnp.int32) // (group_tiles // 3))[None, :]
    row_slot = (my_rows // per_level - above) * owned + my_rows % owned
    col_slot = group * owned + my_cols % owned
    S, B, slots = build_operators(factor_tiles, diag_inv, row_slot, col_slot)

    pairs = [
        [[i, i + 1] for i in range(0, n, 2)],
        [[i, (i + 1) % n] for i in range(1, n, 2)],
    ]
    swaps = [[(p, q) for p, q in g] + [(q, p) for p, q in g] for g in pairs]
    B_far = [lax.ppermute(B[k], "sn", swaps[1 - k % 2]) for k in range(4)]

    def own_op(l):
        which, index = slots[l - 1]
        return B[which], index

    def far_op(l):
        which, index = slots[l - 1]
        return B_far[which], index

    def swap(l, message):
        return lax.all_gather(message, "sn", axis_index_groups=pairs[l % 2])

    def diag_fwd(d_ref, l, f):
        f = f.astype(BF)
        return jnp.concatenate(
            [dot_t(f[:, q * b : (q + 1) * b], d_ref[l, q]) for q in range(owned)], axis=1
        )

    def diag_bwd(d_ref, l, e):
        return jnp.concatenate(
            [dot_n(e[:, q * b : (q + 1) * b], d_ref[l, q]) for q in range(owned)], axis=1
        ).astype(BF)

    def side_of(par_ref, l):
        return par_ref[0] if l % 2 == 0 else 1 - par_ref[0]

    def at(start, size):
        return pl.ds(pl.multiple_of(start, w), size)

    def forward_step(l, message, acc):
        got = swap(l, message)
        b_own, i_own = own_op(l)
        b_par, i_par = far_op(l)
        more, rest_levels = l + 1 < levels, levels - l - 2
        base = 2 * w if l == 1 else 0

        def step(par_ref, g_ref, bo_ref, bp_ref, *rest):
            y4 = rest[-1]
            s = side_of(par_ref, l)
            y4[:, : 2 * w] = g_ref[0, :, : 2 * w]
            y4[:, 2 * w :] = g_ref[1, :, : 2 * w]
            mine = y4[:, at(s * w, 3 * w)]
            theirs = y4[:, at((1 - s) * w, 3 * w)]
            h_own = g_ref[s, :, 2 * w :].astype(F32)
            h_par = g_ref[1 - s, :, 2 * w :].astype(F32)
            m_ref = rest[3] if more else rest[0]
            m_ref[:, at(s * w, w)] = (h_own - dot_t(mine, bo_ref[i_own])).astype(BF)
            m_ref[:, at((1 - s) * w, w)] = (h_par - dot_t(theirs, bp_ref[i_par])).astype(BF)
            if more:
                s_ref, d_ref, acc_ref = rest[:3]
                f = acc_ref[:, base : base + w].astype(F32) - dot_t(mine, s_ref[w : 2 * w, :])
                m_ref[:, 2 * w :] = diag_fwd(d_ref, l + 1, f).astype(BF)
                if rest_levels:
                    rest[4][...] = acc_ref[:, base + w :].astype(F32) - dot_t(mine, s_ref[2 * w :, :])

        args, outs = (parity, got, b_own, b_par), [((cols, 3 * w if more else 2 * w), BF)]
        if more:
            args += (S[l - 1], diag_inv, acc)
            if rest_levels:
                outs.append(((cols, rest_levels * w), F32))
        res = call(step, outs, args, [pltpu.VMEM((cols, 4 * w), BF)])
        return res[0], res[-1]

    def backward_step(l, got, y_pair, older, above):
        b_own, i_own = own_op(l)
        b_par, i_par = far_op(l)
        top, more = l == levels - 1, l >= 2
        args = (parity, y_pair, b_own, b_par, diag_inv)
        if not top:
            args += (got, older)
        if more:
            args += (S[l - 2], *above)
        n_in = len(args)
        outs = [((cols, 3 * w if more else 2 * w), BF), ((cols, w), BF)]
        if more:
            outs.append(((cols, 3 * w), F32))

        def step(*refs):
            par_ref, y_ref, bo_ref, bp_ref, d_ref = refs[:5]
            m_ref, z_ref = refs[n_in : n_in + 2]
            e_ref = refs[-1]
            s = side_of(par_ref, l)
            e = y_ref[:, : 2 * w]
            if not top:
                g_ref, old_ref = refs[5:7]
                e = e.astype(F32) - g_ref[0, :, : 2 * w].astype(F32) - g_ref[1, :, : 2 * w].astype(F32)
            e_ref[...] = e.astype(BF)
            e_own, e_par = e_ref[:, at(s * w, w)], e_ref[:, at((1 - s) * w, w)]
            z_own = diag_bwd(d_ref, l, e_own)
            z_ref[...] = z_own
            part = dot_n(e_own, bo_ref[i_own, :, at(s * w, 2 * w)])
            extra = dot_n(e_par, bp_ref[i_par, :, at(s * 2 * w, w)])
            if not top:
                part = part + old_ref[:, at(s * w, 2 * w)]
                extra = extra + g_ref[1 - s, :, 2 * w :].astype(F32)
            for k in range(2):
                piece = part[:, k * w : (k + 1) * w]
                m_ref[:, k * w : (k + 1) * w] = jnp.where(s == 1 - k, piece + extra, piece).astype(BF)
            if more:
                s_ref, old_out = refs[n_in - 1 - len(above)], refs[n_in + 2]
                total = dot_n(z_own, s_ref[w : 2 * w, :])
                for k, zr in enumerate(refs[n_in - len(above) : n_in]):
                    total = total + dot_n(zr[...], s_ref[(k + 2) * w : (k + 3) * w, :])
                old_out[...] = total
                m_ref[:, 2 * w :] = old_out[:, at(s * 2 * w, w)].astype(BF)

        res = call(step, outs, args, [pltpu.VMEM((cols, 2 * w), BF)])
        return res[0], res[1], res[2] if more else None

    def start(x_ref, d_ref, y_ref, h_ref):
        y_ref[...] = diag_fwd(d_ref, 0, x_ref[:, :w]).astype(BF)
        h_ref[...] = diag_fwd(d_ref, 1, x_ref[:, w : 2 * w]).astype(BF)

    y0, h1 = call(start, [((cols, w), BF)] * 2, (panels, diag_inv))
    both = swap(0, y0)
    message = jnp.concatenate([both[0], both[1], h1], axis=1)

    pair_y = [None] * levels
    acc = panels
    for l in range(1, levels):
        pair_y[l], acc = forward_step(l, message, acc)
        message = pair_y[l]

    z = [None] * levels
    got, older = None, None
    for l in range(levels - 1, 0, -1):
        message, z[l], older = backward_step(l, got, pair_y[l], older, z[l + 1 :])
        got = swap(l - 1, message)

    def finish(par_ref, g_ref, y_ref, d_ref, *rest):
        o_ref = rest[-1]
        here = at(par_ref[0] * w, w)
        terms = g_ref[0, :, here].astype(F32) + g_ref[1, :, here].astype(F32)
        e = (y_ref[...].astype(F32) - terms).astype(BF)
        o_ref[:, :w] = diag_bwd(d_ref, 0, e)
        for k in range(1, levels):
            o_ref[:, k * w : (k + 1) * w] = rest[k - 1][...]

    (combined,) = call(finish, [((cols, levels * w), BF)], (parity, got, y0, diag_inv, *z[1:]))
    combined = combined.reshape(cols, levels, w)
    return lax.all_to_all(combined, "rhs", split_axis=2, concat_axis=0, tiled=True)


def solution(mesh):
    placed = (
        P(None, None, ("sn", "rhs")),
        P(None, "sn", None, None),
        P(None, "sn", None, None),
        P(),
        P(),
    )
    return jax.shard_map(
        on_device,
        mesh=mesh,
        in_specs=placed,
        out_specs=P(None, None, ("sn", "rhs")),
        check_vma=False,
    )
```

```python
import jax
import jax.numpy as jnp
from jax import lax
from jax.experimental import pallas as pl
from jax.experimental.pallas import tpu as pltpu
from jax.sharding import PartitionSpec as P

BF = jnp.bfloat16
F32 = jnp.float32
VMEM = pl.BlockSpec(memory_space=pltpu.VMEM)
SMEM = pl.BlockSpec(memory_space=pltpu.SMEM)
HBM = pl.BlockSpec(memory_space=pltpu.HBM)


def dot_t(a, w):
    return lax.dot_general(a, w, (((1,), (1,)), ((), ())), preferred_element_type=F32)


def dot_n(a, w):
    return lax.dot_general(a, w, (((1,), (0,)), ((), ())), preferred_element_type=F32)


def call(body, outs, args, scratch=(), flops=10**7, mib=12, out_specs=None, size=None):
    specs = [SMEM if a.dtype == jnp.int32 else VMEM for a in args]
    if size is None:
        size = sum(a.size * a.dtype.itemsize for a in args)
    return pl.pallas_call(
        body,
        out_shape=[jax.ShapeDtypeStruct(s, d) for s, d in outs],
        in_specs=specs,
        out_specs=out_specs or [VMEM] * len(outs),
        scratch_shapes=list(scratch),
        compiler_params=pltpu.CompilerParams(vmem_limit_bytes=mib * 2**20),
        cost_estimate=pl.CostEstimate(flops=flops, bytes_accessed=size, transcendentals=0),
    )(*args)


def build_operators(tiles, diag, row_slot, col_slot, parity, side_of):
    levels, owned, b, _ = diag.shape
    count = tiles.shape[1]
    tall = owned * b
    wide = 3 * tall

    def body(row_ref, col_ref, par_ref, t_ref, d_ref, *refs):
        outs, (scratch, sems) = refs[: 2 * levels], refs[2 * levels :]
        s_out, b_out, sends = outs[: levels - 1], outs[levels - 1 : 2 * levels - 2], outs[-2:]
        copies = []
        for l in range(levels - 1):
            size = (levels - 1 - l) * tall
            start = sum((levels - 1 - k) * tall for k in range(l))
            buf = scratch.at[pl.ds(start, size), :]
            buf[...] = jnp.zeros((size, wide), BF)

            def add(t, carry):
                r = pl.multiple_of(row_ref[l, t] * b, b)
                c = pl.multiple_of(col_ref[l, t] * b, b)
                at = (pl.ds(r, b), pl.ds(c, b))
                buf[at] = buf[at] + t_ref[l, t]
                return carry

            lax.fori_loop(0, count, add, 0, unroll=8)
            copies.append(pltpu.make_async_copy(buf, s_out[l], sems.at[l]))
            copies[-1].start()
            for q in range(owned):
                rows = slice(q * b, (q + 1) * b)
                b_out[l][rows, :] = dot_n(d_ref[l + 1, q], buf[rows, :]).astype(BF)
            s = side_of(par_ref, l + 1)
            toward = pl.ds(pl.multiple_of((1 - s) * 2 * tall, tall), tall)
            sends[l % 2][l // 2] = b_out[l][:, toward]
        for c in copies:
            c.wait()

    outs = [(((levels - 1 - l) * tall, wide), BF) for l in range(levels - 1)]
    outs += [((tall, wide), BF)] * (levels - 1)
    outs += [((levels // 2, tall, tall), BF), (((levels - 1) // 2, tall, tall), BF)]
    res = call(
        body,
        outs,
        (row_slot, col_slot, parity, tiles, diag),
        [
            pltpu.VMEM((levels * (levels - 1) // 2 * tall, wide), BF),
            pltpu.SemaphoreType.DMA((levels - 1,)),
        ],
        mib=40,
        out_specs=[HBM] * (levels - 1) + [VMEM] * (levels + 1),
        size=2**10,
    )
    return res[: levels - 1], res[levels - 1 : 2 * levels - 2], res[-2:]


def on_device(lanczos_block, diag_inv, factor_tiles, tile_rows, tile_cols):
    levels, owned, b = diag_inv.shape[:3]
    group_tiles = factor_tiles.shape[1]
    n = lax.axis_size("sn")
    peers = lax.axis_size("rhs")
    own = lax.axis_index("sn")
    per_level = owned * n
    w = owned * b
    total, _, piece = lanczos_block.shape
    cols = total // peers
    parity = (own % 2).astype(jnp.int32).reshape(1)

    def side_of(par_ref, l):
        return par_ref[0] if l % 2 == 0 else 1 - par_ref[0]

    def pack(x_ref, o_ref):
        rows = [x_ref[pl.ds(k, total, stride=levels), :] for k in range(levels)]
        v = jnp.concatenate(rows, axis=1).astype(BF)
        for j in range(peers):
            o_ref[j] = v[j * cols : (j + 1) * cols]

    (sent,) = call(pack, [((peers, cols, levels * piece), BF)], (lanczos_block.reshape(total * levels, piece),))
    arrived = lax.all_to_all(sent, "rhs", split_axis=0, concat_axis=0, tiled=True)

    my_rows = lax.dynamic_slice_in_dim(tile_rows, own * group_tiles, group_tiles, 1)
    my_cols = lax.dynamic_slice_in_dim(tile_cols, own * group_tiles, group_tiles, 1)
    above = jnp.arange(1, levels, dtype=jnp.int32)[:, None]
    group = (jnp.arange(group_tiles, dtype=jnp.int32) // (group_tiles // 3))[None, :]
    row_slot = (my_rows // per_level - above) * owned + my_rows % owned
    col_slot = group * owned + my_cols % owned
    sent, factor_tiles = lax.optimization_barrier((sent, factor_tiles))
    S, B, toward = build_operators(factor_tiles, diag_inv, row_slot, col_slot, parity, side_of)

    pairs = [
        [[i, i + 1] for i in range(0, n, 2)],
        [[i, (i + 1) % n] for i in range(1, n, 2)],
    ]
    swaps = [[(p, q) for p, q in g] + [(q, p) for p, q in g] for g in pairs]
    far_odd, far_even = (lax.ppermute(toward[k], "sn", swaps[1 - k]) for k in range(2))
    far = [None] + [(far_odd if l % 2 else far_even)[(l - 1) // 2] for l in range(1, levels)]

    def swap(l, message):
        return lax.all_gather(message, "sn", axis_index_groups=pairs[l % 2])

    def diag_fwd(d_ref, l, f):
        f = f.astype(BF)
        return jnp.concatenate(
            [dot_t(f[:, q * b : (q + 1) * b], d_ref[l, q]) for q in range(owned)], axis=1
        )

    def diag_bwd(d_ref, l, e):
        return jnp.concatenate(
            [dot_n(e[:, q * b : (q + 1) * b], d_ref[l, q]) for q in range(owned)], axis=1
        ).astype(BF)

    def at(start, size):
        return pl.ds(pl.multiple_of(start, w), size)

    def unpack(a_ref, d_ref, x_ref, y_ref):
        for k in range(levels):
            parts = [a_ref[j].astype(F32)[:, k * piece : (k + 1) * piece] for j in range(peers)]
            x_ref[:, k * w : (k + 1) * w] = jnp.concatenate(parts, axis=1)
        y_ref[...] = diag_fwd(d_ref, 0, x_ref[:, :w]).astype(BF)

    x, y0 = call(unpack, [((cols, levels * w), F32), ((cols, w), BF)], (arrived, diag_inv))

    def forward_step(l, got, before, acc):
        more, rest_levels = l + 1 < levels, levels - l - 2
        base = 2 * w if l == 1 else (w if l == 0 else 0)
        args, outs = (parity, got), [((cols, 2 * w), BF)]
        if l:
            args += (B[l - 1], far[l])
        if more:
            args += (B[l], diag_inv, acc)
            outs.append(((cols, 2 * w), BF))
            if l:
                args += (S[l - 1], before)
                if rest_levels:
                    outs.append(((cols, rest_levels * w), F32))
        n_in = len(args)

        def step(*refs):
            par_ref, g_ref = refs[:2]
            p_ref, y3 = refs[n_in], refs[-1]
            s = side_of(par_ref, l)
            if l:
                near_ref, far_ref = refs[2:4]
                y_own, y_par = g_ref[s, :, w:], g_ref[1 - s, :, w:]
                q_own, q_par = g_ref[s, :, :w].astype(F32), g_ref[1 - s, :, :w].astype(F32)
                new = (q_own - dot_t(y_par, near_ref[:, at((1 - s) * 2 * w, w)])).astype(BF)
                p_ref[:, at(s * w, w)] = new
                p_ref[:, at((1 - s) * w, w)] = (q_par - dot_t(y_own, far_ref[...])).astype(BF)
            else:
                p_ref[:, :w] = g_ref[0]
                p_ref[:, w:] = g_ref[1]
                new = g_ref[s]
            if not more:
                return
            m_ref = refs[n_in + 1]
            m_ref[:, w:] = new
            k = 4 if l else 2
            next_ref, d_ref, acc_ref = refs[k : k + 3]
            f = acc_ref[:, base : base + w]
            if l:
                s_ref, before_ref = refs[k + 3 : k + 5]
                y3[:, at(s * w, 2 * w)] = before_ref[...]
                y3[:, at((1 - s) * 2 * w, w)] = y_par
                f = f - dot_t(y3[...], s_ref[w : 2 * w, :])
            h = diag_fwd(d_ref, l + 1, f)
            q = h - dot_t(p_ref[...], next_ref[:, at((1 - s) * w, 2 * w)])
            m_ref[:, :w] = q.astype(BF)
            if l and rest_levels:
                refs[n_in + 2][...] = acc_ref[:, base + w :] - dot_t(y3[...], s_ref[2 * w :, :])

        res = call(step, outs, args, [pltpu.VMEM((cols, 3 * w), BF)])
        return res[0], res[1] if more else None, res[-1] if l else acc

    pair_y = [None] * levels
    acc, message, before = x, y0, None
    for l in range(levels):
        before, message, acc = forward_step(l, swap(l, message), before, acc)
        pair_y[l] = before

    def backward_step(l, got, older, above):
        top, more = l == levels - 1, l >= 2
        args = (parity, pair_y[l], B[l - 1], far[l], diag_inv)
        if not top:
            args += (got, older)
        if more:
            args += (S[l - 2], *above)
        n_in = len(args)
        outs = [((cols, 3 * w if more else 2 * w), BF), ((cols, w), BF)]
        if more:
            outs.append(((cols, 3 * w), F32))

        def step(*refs):
            par_ref, y_ref, near_ref, far_ref, d_ref = refs[:5]
            m_ref, z_ref = refs[n_in : n_in + 2]
            e_ref = refs[-1]
            s = side_of(par_ref, l)
            e = y_ref[...]
            if not top:
                g_ref, old_ref = refs[5:7]
                e = e.astype(F32) - g_ref[0, :, : 2 * w].astype(F32) - g_ref[1, :, : 2 * w].astype(F32)
            e_ref[...] = e.astype(BF)
            e_own, e_par = e_ref[:, at(s * w, w)], e_ref[:, at((1 - s) * w, w)]
            z_own = diag_bwd(d_ref, l, e_own)
            z_ref[...] = z_own
            part = dot_n(e_own, near_ref[:, at(s * w, 2 * w)])
            extra = dot_n(e_par, far_ref[...])
            if not top:
                part = part + old_ref[:, at(s * w, 2 * w)]
                extra = extra + g_ref[1 - s, :, 2 * w :].astype(F32)
            for k in range(2):
                half = part[:, k * w : (k + 1) * w]
                m_ref[:, k * w : (k + 1) * w] = jnp.where(s == 1 - k, half + extra, half).astype(BF)
            if more:
                s_ref, old_out = refs[n_in - 1 - len(above)], refs[n_in + 2]
                sums = dot_n(z_own, s_ref[w : 2 * w, :])
                for k, zr in enumerate(refs[n_in - len(above) : n_in]):
                    sums = sums + dot_n(zr[...], s_ref[(k + 2) * w : (k + 3) * w, :])
                old_out[...] = sums
                m_ref[:, 2 * w :] = old_out[:, at(s * 2 * w, w)].astype(BF)

        res = call(step, outs, args, [pltpu.VMEM((cols, 2 * w), BF)])
        return res[0], res[1], res[2] if more else None

    z = [None] * levels
    got, older = None, None
    for l in range(levels - 1, 0, -1):
        message, z[l], older = backward_step(l, got, older, z[l + 1 :])
        got = swap(l - 1, message)

    def finish(par_ref, g_ref, y_ref, d_ref, *rest):
        o_ref = rest[-1]
        here = at(par_ref[0] * w, w)
        terms = g_ref[0, :, here].astype(F32) + g_ref[1, :, here].astype(F32)
        e = (y_ref[...].astype(F32) - terms).astype(BF)
        values = [diag_bwd(d_ref, 0, e).astype(F32)] + [r[...].astype(F32) for r in rest[:-1]]
        for j in range(peers):
            parts = [v[:, j * piece : (j + 1) * piece] for v in values]
            o_ref[j] = jnp.concatenate(parts, axis=1).astype(BF)

    (result,) = call(finish, [((peers, cols, levels * piece), BF)], (parity, got, y0, diag_inv, *z[1:]))
    result = lax.all_to_all(result, "rhs", split_axis=0, concat_axis=0, tiled=True)
    return result.reshape(total, levels, piece)


def solution(mesh):
    placed = (
        P(None, None, ("sn", "rhs")),
        P(None, "sn", None, None),
        P(None, "sn", None, None),
        P(),
        P(),
    )
    return jax.shard_map(
        on_device,
        mesh=mesh,
        in_specs=placed,
        out_specs=P(None, None, ("sn", "rhs")),
        check_vma=False,
    )
```

```python
import jax
import jax.numpy as jnp
from jax import lax
from jax.experimental import pallas as pl
from jax.experimental.pallas import tpu as pltpu
from jax.sharding import PartitionSpec as P

BF = jnp.bfloat16
F32 = jnp.float32
VMEM = pl.BlockSpec(memory_space=pltpu.VMEM)
SMEM = pl.BlockSpec(memory_space=pltpu.SMEM)
HBM = pl.BlockSpec(memory_space=pltpu.HBM)


def dot_t(a, w):
    return lax.dot_general(a, w, (((1,), (1,)), ((), ())), preferred_element_type=F32)


def dot_n(a, w):
    return lax.dot_general(a, w, (((1,), (0,)), ((), ())), preferred_element_type=F32)


def call(body, outs, args, scratch=(), flops=10**7, mib=12, specs=None, out_specs=None, size=None):
    specs = specs or [SMEM if a.dtype == jnp.int32 else VMEM for a in args]
    if size is None:
        size = sum(a.size * a.dtype.itemsize for a in args)
    return pl.pallas_call(
        body,
        out_shape=[jax.ShapeDtypeStruct(s, d) for s, d in outs],
        in_specs=specs,
        out_specs=out_specs or [VMEM] * len(outs),
        scratch_shapes=list(scratch),
        compiler_params=pltpu.CompilerParams(vmem_limit_bytes=mib * 2**20),
        cost_estimate=pl.CostEstimate(flops=flops, bytes_accessed=size, transcendentals=0),
    )(*args)


def build_operators(tiles, diag, row_slot, col_slot, parity, side_of):
    levels, owned, b, _ = diag.shape
    count = tiles.shape[1]
    tall = owned * b
    wide = 3 * tall

    def body(row_ref, col_ref, par_ref, t_ref, d_ref, *refs):
        outs, (scratch, held, sems, in_sems) = refs[: 2 * levels], refs[2 * levels :]
        s_out, b_out, sends = outs[: levels - 1], outs[levels - 1 : 2 * levels - 2], outs[-2:]
        loads = [
            pltpu.make_async_copy(t_ref.at[l], held.at[l], in_sems.at[l]) for l in range(levels - 1)
        ]
        for c in loads:
            c.start()
        copies = []
        for l in range(levels - 1):
            size = (levels - 1 - l) * tall
            start = sum((levels - 1 - k) * tall for k in range(l))
            buf = scratch.at[pl.ds(start, size), :]
            buf[...] = jnp.zeros((size, wide), BF)
            loads[l].wait()

            def add(t, carry):
                r = pl.multiple_of(row_ref[l, t] * b, b)
                c = pl.multiple_of(col_ref[l, t] * b, b)
                at = (pl.ds(r, b), pl.ds(c, b))
                buf[at] = buf[at] + held[l, t]
                return carry

            lax.fori_loop(0, count, add, 0, unroll=8)
            copies.append(pltpu.make_async_copy(buf, s_out[l], sems.at[l]))
            copies[-1].start()
            for q in range(owned):
                rows = slice(q * b, (q + 1) * b)
                b_out[l][rows, :] = dot_n(d_ref[l + 1, q], buf[rows, :]).astype(BF)
            s = side_of(par_ref, l + 1)
            toward = pl.ds(pl.multiple_of((1 - s) * 2 * tall, tall), tall)
            sends[l % 2][l // 2] = b_out[l][:, toward]
        for c in copies:
            c.wait()

    outs = [(((levels - 1 - l) * tall, wide), BF) for l in range(levels - 1)]
    outs += [((tall, wide), BF)] * (levels - 1)
    outs += [((levels // 2, tall, tall), BF), (((levels - 1) // 2, tall, tall), BF)]
    res = call(
        body,
        outs,
        (row_slot, col_slot, parity, tiles, diag),
        [
            pltpu.VMEM((levels * (levels - 1) // 2 * tall, wide), BF),
            pltpu.VMEM(tiles.shape, BF),
            pltpu.SemaphoreType.DMA((levels - 1,)),
            pltpu.SemaphoreType.DMA((levels - 1,)),
        ],
        flops=4 * 10**8,
        mib=60,
        specs=[SMEM, SMEM, SMEM, HBM, VMEM],
        out_specs=[HBM] * (levels - 1) + [VMEM] * (levels + 1),
        size=24 * 2**20,
    )
    return res[: levels - 1], res[levels - 1 : 2 * levels - 2], res[-2:]


def on_device(lanczos_block, diag_inv, factor_tiles, tile_rows, tile_cols):
    levels, owned, b = diag_inv.shape[:3]
    group_tiles = factor_tiles.shape[1]
    n = lax.axis_size("sn")
    peers = lax.axis_size("rhs")
    own = lax.axis_index("sn")
    per_level = owned * n
    w = owned * b
    total, _, piece = lanczos_block.shape
    cols = total // peers
    parity = (own % 2).astype(jnp.int32).reshape(1)

    def side_of(par_ref, l):
        return par_ref[0] if l % 2 == 0 else 1 - par_ref[0]

    def pack(x_ref, o_ref):
        v = x_ref[...].T.astype(BF)
        for j in range(peers):
            o_ref[j] = v[j * cols : (j + 1) * cols]

    flat = lanczos_block.transpose(1, 2, 0).reshape(levels * piece, total)
    (sent,) = call(pack, [((peers, cols, levels * piece), BF)], (flat,))
    arrived = lax.all_to_all(sent, "rhs", split_axis=0, concat_axis=0, tiled=True)

    my_rows = lax.dynamic_slice_in_dim(tile_rows, own * group_tiles, group_tiles, 1)
    my_cols = lax.dynamic_slice_in_dim(tile_cols, own * group_tiles, group_tiles, 1)
    above = jnp.arange(1, levels, dtype=jnp.int32)[:, None]
    group = (jnp.arange(group_tiles, dtype=jnp.int32) // (group_tiles // 3))[None, :]
    row_slot = (my_rows // per_level - above) * owned + my_rows % owned
    col_slot = group * owned + my_cols % owned
    sent, factor_tiles = lax.optimization_barrier((sent, factor_tiles))
    S, B, toward = build_operators(factor_tiles, diag_inv, row_slot, col_slot, parity, side_of)

    pairs = [
        [[i, i + 1] for i in range(0, n, 2)],
        [[i, (i + 1) % n] for i in range(1, n, 2)],
    ]
    swaps = [[(p, q) for p, q in g] + [(q, p) for p, q in g] for g in pairs]
    arrived, toward = lax.optimization_barrier((arrived, list(toward)))
    far_odd, far_even = (lax.ppermute(toward[k], "sn", swaps[1 - k]) for k in range(2))
    far = [None] + [(far_odd if l % 2 else far_even)[(l - 1) // 2] for l in range(1, levels)]

    def swap(l, message):
        return lax.all_gather(message, "sn", axis_index_groups=pairs[l % 2])

    def diag_fwd(d_ref, l, f):
        f = f.astype(BF)
        return jnp.concatenate(
            [dot_t(f[:, q * b : (q + 1) * b], d_ref[l, q]) for q in range(owned)], axis=1
        )

    def diag_bwd(d_ref, l, e):
        return jnp.concatenate(
            [dot_n(e[:, q * b : (q + 1) * b], d_ref[l, q]) for q in range(owned)], axis=1
        ).astype(BF)

    def at(start, size):
        return pl.ds(pl.multiple_of(start, w), size)

    def unpack(a_ref, d_ref, x_ref, y_ref):
        for k in range(levels):
            parts = [a_ref[j].astype(F32)[:, k * piece : (k + 1) * piece] for j in range(peers)]
            x_ref[:, k * w : (k + 1) * w] = jnp.concatenate(parts, axis=1)
        y_ref[...] = diag_fwd(d_ref, 0, x_ref[:, :w]).astype(BF)

    x, y0 = call(unpack, [((cols, levels * w), F32), ((cols, w), BF)], (arrived, diag_inv))

    def forward_step(l, got, before, acc):
        more, rest_levels = l + 1 < levels, levels - l - 2
        base = 2 * w if l == 1 else (w if l == 0 else 0)
        args, outs = (parity, got), [((cols, 2 * w), BF)]
        if l:
            args += (B[l - 1], far[l])
        if more:
            args += (B[l], diag_inv, acc)
            outs.append(((cols, 2 * w), BF))
            if l:
                args += (S[l - 1], before)
                if rest_levels:
                    outs.append(((cols, rest_levels * w), F32))
        n_in = len(args)

        def step(*refs):
            par_ref, g_ref = refs[:2]
            p_ref, y3 = refs[n_in], refs[-1]
            s = side_of(par_ref, l)
            if l:
                near_ref, far_ref = refs[2:4]
                y_own, y_par = g_ref[s, :, w:], g_ref[1 - s, :, w:]
                q_own, q_par = g_ref[s, :, :w].astype(F32), g_ref[1 - s, :, :w].astype(F32)
                new = (q_own - dot_t(y_par, near_ref[:, at((1 - s) * 2 * w, w)])).astype(BF)
                p_ref[:, at(s * w, w)] = new
                p_ref[:, at((1 - s) * w, w)] = (q_par - dot_t(y_own, far_ref[...])).astype(BF)
            else:
                p_ref[:, :w] = g_ref[0]
                p_ref[:, w:] = g_ref[1]
                new = g_ref[s]
            if not more:
                return
            m_ref = refs[n_in + 1]
            m_ref[:, w:] = new
            k = 4 if l else 2
            next_ref, d_ref, acc_ref = refs[k : k + 3]
            f = acc_ref[:, base : base + w]
            if l:
                s_ref, before_ref = refs[k + 3 : k + 5]
                y3[:, at(s * w, 2 * w)] = before_ref[...]
                y3[:, at((1 - s) * 2 * w, w)] = y_par
                f = f - dot_t(y3[...], s_ref[w : 2 * w, :])
            h = diag_fwd(d_ref, l + 1, f)
            q = h - dot_t(p_ref[...], next_ref[:, at((1 - s) * w, 2 * w)])
            m_ref[:, :w] = q.astype(BF)
            if l and rest_levels:
                refs[n_in + 2][...] = acc_ref[:, base + w :] - dot_t(y3[...], s_ref[2 * w :, :])

        res = call(step, outs, args, [pltpu.VMEM((cols, 3 * w), BF)])
        return res[0], res[1] if more else None, res[-1] if l else acc

    pair_y = [None] * levels
    acc, message, before = x, y0, None
    for l in range(levels):
        before, message, acc = forward_step(l, swap(l, message), before, acc)
        pair_y[l] = before

    def backward_step(l, got, older, above):
        top, more = l == levels - 1, l >= 2
        args = (parity, pair_y[l], B[l - 1], far[l], diag_inv)
        if not top:
            args += (got, older)
        if more:
            args += (S[l - 2], *above)
        n_in = len(args)
        outs = [((cols, 3 * w if more else 2 * w), BF), ((cols, w), BF)]
        if more:
            outs.append(((cols, 3 * w), F32))

        def step(*refs):
            par_ref, y_ref, near_ref, far_ref, d_ref = refs[:5]
            m_ref, z_ref = refs[n_in : n_in + 2]
            e_ref = refs[-1]
            s = side_of(par_ref, l)
            e = y_ref[...]
            if not top:
                g_ref, old_ref = refs[5:7]
                e = e.astype(F32) - g_ref[0, :, : 2 * w].astype(F32) - g_ref[1, :, : 2 * w].astype(F32)
            e_ref[...] = e.astype(BF)
            e_own, e_par = e_ref[:, at(s * w, w)], e_ref[:, at((1 - s) * w, w)]
            z_own = diag_bwd(d_ref, l, e_own)
            z_ref[...] = z_own
            part = dot_n(e_own, near_ref[:, at(s * w, 2 * w)])
            extra = dot_n(e_par, far_ref[...])
            if not top:
                part = part + old_ref[:, at(s * w, 2 * w)]
                extra = extra + g_ref[1 - s, :, 2 * w :].astype(F32)
            for k in range(2):
                half = part[:, k * w : (k + 1) * w]
                m_ref[:, k * w : (k + 1) * w] = jnp.where(s == 1 - k, half + extra, half).astype(BF)
            if more:
                s_ref, old_out = refs[n_in - 1 - len(above)], refs[n_in + 2]
                sums = dot_n(z_own, s_ref[w : 2 * w, :])
                for k, zr in enumerate(refs[n_in - len(above) : n_in]):
                    sums = sums + dot_n(zr[...], s_ref[(k + 2) * w : (k + 3) * w, :])
                old_out[...] = sums
                m_ref[:, 2 * w :] = old_out[:, at(s * 2 * w, w)].astype(BF)

        res = call(step, outs, args, [pltpu.VMEM((cols, 2 * w), BF)])
        return res[0], res[1], res[2] if more else None

    z = [None] * levels
    got, older = None, None
    for l in range(levels - 1, 0, -1):
        message, z[l], older = backward_step(l, got, older, z[l + 1 :])
        got = swap(l - 1, message)

    def finish(par_ref, g_ref, y_ref, d_ref, *rest):
        o_ref = rest[-1]
        here = at(par_ref[0] * w, w)
        terms = g_ref[0, :, here].astype(F32) + g_ref[1, :, here].astype(F32)
        e = (y_ref[...].astype(F32) - terms).astype(BF)
        values = [diag_bwd(d_ref, 0, e).astype(F32)] + [r[...].astype(F32) for r in rest[:-1]]
        for j in range(peers):
            parts = [v[:, j * piece : (j + 1) * piece] for v in values]
            o_ref[j] = jnp.concatenate(parts, axis=1).astype(BF)

    (result,) = call(finish, [((peers, cols, levels * piece), BF)], (parity, got, y0, diag_inv, *z[1:]))
    result = lax.all_to_all(result, "rhs", split_axis=0, concat_axis=0, tiled=True)

    def turn(r_ref, o_ref):
        for j in range(peers):
            o_ref[:, j * cols : (j + 1) * cols] = r_ref[j].astype(F32).T.astype(BF)

    (result,) = call(turn, [((levels * piece, total), BF)], (result,))
    return result.reshape(levels, piece, total).transpose(2, 0, 1)


def solution(mesh):
    placed = (
        P(None, None, ("sn", "rhs")),
        P(None, "sn", None, None),
        P(None, "sn", None, None),
        P(),
        P(),
    )
    return jax.shard_map(
        on_device,
        mesh=mesh,
        in_specs=placed,
        out_specs=P(None, None, ("sn", "rhs")),
        check_vma=False,
    )
```

```python
import jax
import jax.numpy as jnp
from jax import lax
from jax.experimental import pallas as pl
from jax.experimental.pallas import tpu as pltpu
from jax.sharding import PartitionSpec as P

BF = jnp.bfloat16
F32 = jnp.float32
VMEM = pl.BlockSpec(memory_space=pltpu.VMEM)
SMEM = pl.BlockSpec(memory_space=pltpu.SMEM)
HBM = pl.BlockSpec(memory_space=pltpu.HBM)


def dot_t(a, w):
    return lax.dot_general(a, w, (((1,), (1,)), ((), ())), preferred_element_type=F32)


def dot_n(a, w):
    return lax.dot_general(a, w, (((1,), (0,)), ((), ())), preferred_element_type=F32)


def call(body, outs, args, scratch=(), flops=10**7, mib=12, specs=None, out_specs=None, size=None, aliases=None):
    specs = specs or [SMEM if a.dtype == jnp.int32 else VMEM for a in args]
    if size is None:
        size = sum(a.size * a.dtype.itemsize for a in args)
    return pl.pallas_call(
        body,
        out_shape=[jax.ShapeDtypeStruct(s, d) for s, d in outs],
        in_specs=specs,
        out_specs=out_specs or [VMEM] * len(outs),
        scratch_shapes=list(scratch),
        input_output_aliases=aliases or {},
        compiler_params=pltpu.CompilerParams(vmem_limit_bytes=mib * 2**20),
        cost_estimate=pl.CostEstimate(flops=flops, bytes_accessed=size, transcendentals=0),
    )(*args)


def build_operators(tiles, diag, row_slot, col_slot, place, side_of):
    levels, owned, b, _ = diag.shape
    count = tiles.shape[1]
    tall = owned * b
    wide = 3 * tall

    def body(row_ref, col_ref, par_ref, t_ref, d_ref, *refs):
        outs, (scratch, held, sems, in_sems) = refs[: 2 * levels - 1], refs[2 * levels - 1 :]
        s_out, b_out, send = outs[: levels - 1], outs[levels - 1 : 2 * levels - 2], outs[-1]
        loads = [
            pltpu.make_async_copy(t_ref.at[l], held.at[l], in_sems.at[l]) for l in range(levels - 1)
        ]
        for c in loads:
            c.start()
        copies = []
        for l in range(levels - 1):
            size = (levels - 1 - l) * tall
            start = sum((levels - 1 - k) * tall for k in range(l))
            buf = scratch.at[pl.ds(start, size), :]
            buf[...] = jnp.zeros((size, wide), BF)
            loads[l].wait()

            def add(t, carry):
                r = pl.multiple_of(row_ref[l, t] * b, b)
                c = pl.multiple_of(col_ref[l, t] * b, b)
                at = (pl.ds(r, b), pl.ds(c, b))
                buf[at] = buf[at] + held[l, t]
                return carry

            lax.fori_loop(0, count, add, 0, unroll=8)
            copies.append(pltpu.make_async_copy(buf, s_out[l], sems.at[l]))
            copies[-1].start()
            for q in range(owned):
                rows = slice(q * b, (q + 1) * b)
                b_out[l][rows, :] = dot_n(d_ref[l + 1, q], buf[rows, :]).astype(BF)
            s = side_of(par_ref, l + 1)
            toward = pl.ds(pl.multiple_of((1 - s) * 2 * tall, tall), tall)

            @pl.when(par_ref[1] == (l + 1) % 2)
            def _():
                send[l // 2] = b_out[l][:, toward]

        @pl.when(par_ref[1] == 0)
        def _():
            send[levels // 2 - 1] = jnp.zeros((tall, tall), BF)

        for c in copies:
            c.wait()

    outs = [(((levels - 1 - l) * tall, wide), BF) for l in range(levels - 1)]
    outs += [((tall, wide), BF)] * (levels - 1)
    outs += [((levels // 2, tall, tall), BF)]
    res = call(
        body,
        outs,
        (row_slot, col_slot, place, tiles, diag),
        [
            pltpu.VMEM((levels * (levels - 1) // 2 * tall, wide), BF),
            pltpu.VMEM(tiles.shape, BF),
            pltpu.SemaphoreType.DMA((levels - 1,)),
            pltpu.SemaphoreType.DMA((levels - 1,)),
        ],
        flops=4 * 10**8,
        mib=60,
        specs=[SMEM, SMEM, SMEM, HBM, VMEM],
        out_specs=[HBM] * (levels - 1) + [VMEM] * levels,
        size=24 * 2**20,
    )
    return res[: levels - 1], res[levels - 1 : 2 * levels - 2], res[-1]


def on_device(lanczos_block, diag_inv, factor_tiles, tile_rows, tile_cols):
    levels, owned, b = diag_inv.shape[:3]
    group_tiles = factor_tiles.shape[1]
    n = lax.axis_size("sn")
    peers = lax.axis_size("rhs")
    own = lax.axis_index("sn")
    per_level = owned * n
    w = owned * b
    total, _, piece = lanczos_block.shape
    cols = total // peers
    core = lax.axis_index("rhs") % 2
    parity = (own % 2).astype(jnp.int32).reshape(1)
    place = jnp.stack([own % 2, core]).astype(jnp.int32)

    def side_of(par_ref, l):
        return par_ref[0] if l % 2 == 0 else 1 - par_ref[0]

    my_rows = lax.dynamic_slice_in_dim(tile_rows, own * group_tiles, group_tiles, 1)
    my_cols = lax.dynamic_slice_in_dim(tile_cols, own * group_tiles, group_tiles, 1)
    above = jnp.arange(1, levels, dtype=jnp.int32)[:, None]
    group = (jnp.arange(group_tiles, dtype=jnp.int32) // (group_tiles // 3))[None, :]
    row_slot = (my_rows // per_level - above) * owned + my_rows % owned
    col_slot = group * owned + my_cols % owned
    def pack(x_ref, o_ref):
        v = x_ref[...].T.astype(BF)
        for j in range(peers):
            o_ref[j] = v[j * cols : (j + 1) * cols]

    flat = lanczos_block.transpose(1, 2, 0).reshape(levels * piece, total)
    (sent,) = call(pack, [((peers, cols, levels * piece), BF)], (flat,))
    arrived = lax.all_to_all(sent, "rhs", split_axis=0, concat_axis=0, tiled=True)

    sent, factor_tiles = lax.optimization_barrier((sent, factor_tiles))
    S, B, toward = build_operators(factor_tiles, diag_inv, row_slot, col_slot, place, side_of)

    pairs = [
        [[i, i + 1] for i in range(0, n, 2)],
        [[i, (i + 1) % n] for i in range(1, n, 2)],
    ]
    arrived, toward = lax.optimization_barrier((arrived, toward))
    partner = [{p: q for g in pairs[k] for p, q in (g, g[::-1])} for k in range(2)]
    fetch = [(i * peers + r, partner[r % 2][i] * peers + r) for i in range(n) for r in range(peers)]
    fetched = lax.ppermute(toward, ("sn", "rhs"), fetch)

    def swap(l, message):
        return lax.all_gather(message, "sn", axis_index_groups=pairs[l % 2])

    def diag_fwd(d_ref, l, f):
        f = f.astype(BF)
        return jnp.concatenate(
            [dot_t(f[:, q * b : (q + 1) * b], d_ref[l, q]) for q in range(owned)], axis=1
        )

    def diag_bwd(d_ref, l, e):
        return jnp.concatenate(
            [dot_n(e[:, q * b : (q + 1) * b], d_ref[l, q]) for q in range(owned)], axis=1
        ).astype(BF)

    def at(start, size):
        return pl.ds(pl.multiple_of(start, w), size)

    def unpack(a_ref, d_ref, x_ref, y_ref):
        for k in range(levels):
            parts = [a_ref[j].astype(F32)[:, k * piece : (k + 1) * piece] for j in range(peers)]
            x_ref[:, k * w : (k + 1) * w] = jnp.concatenate(parts, axis=1)
        y_ref[...] = diag_fwd(d_ref, 0, x_ref[:, :w]).astype(BF)

    x, y0 = call(unpack, [((cols, levels * w), F32), ((cols, w), BF)], (arrived, diag_inv))

    def forward_step(l, got, before, acc):
        more, rest_levels = l + 1 < levels, levels - l - 2
        base = 2 * w if l == 1 else (w if l == 0 else 0)
        args, outs = (parity, got), [((cols, 2 * w), BF)]
        if l:
            args += (B[l - 1], far[l])
        if more:
            args += (B[l], diag_inv, acc)
            outs.append(((cols, 2 * w), BF))
            if l:
                args += (S[l - 1], before)
                if rest_levels:
                    outs.append(((cols, rest_levels * w), F32))
        aliases, extra = {}, {}
        if l == 0:
            aliases, extra = {len(args): len(outs)}, {len(args): pl.BlockSpec(memory_space=pl.ANY)}
            args += (fetched,)
            outs.append((fetched.shape, BF))
        n_in = len(args)

        def step(*refs):
            par_ref, g_ref = refs[:2]
            p_ref, y3 = refs[n_in], refs[-1]
            s = side_of(par_ref, l)
            if l:
                near_ref, far_ref = refs[2:4]
                y_own, y_par = g_ref[s, :, w:], g_ref[1 - s, :, w:]
                q_own, q_par = g_ref[s, :, :w].astype(F32), g_ref[1 - s, :, :w].astype(F32)
                new = (q_own - dot_t(y_par, near_ref[:, at((1 - s) * 2 * w, w)])).astype(BF)
                p_ref[:, at(s * w, w)] = new
                p_ref[:, at((1 - s) * w, w)] = (q_par - dot_t(y_own, far_ref[...])).astype(BF)
            else:
                p_ref[:, :w] = g_ref[0]
                p_ref[:, w:] = g_ref[1]
                new = g_ref[s]
            if not more:
                return
            m_ref = refs[n_in + 1]
            m_ref[:, w:] = new
            k = 4 if l else 2
            next_ref, d_ref, acc_ref = refs[k : k + 3]
            f = acc_ref[:, base : base + w]
            if l:
                s_ref, before_ref = refs[k + 3 : k + 5]
                y3[:, at(s * w, 2 * w)] = before_ref[...]
                y3[:, at((1 - s) * 2 * w, w)] = y_par
                f = f - dot_t(y3[...], s_ref[w : 2 * w, :])
            h = diag_fwd(d_ref, l + 1, f)
            q = h - dot_t(p_ref[...], next_ref[:, at((1 - s) * w, 2 * w)])
            m_ref[:, :w] = q.astype(BF)
            if l and rest_levels:
                refs[n_in + 2][...] = acc_ref[:, base + w :] - dot_t(y3[...], s_ref[2 * w :, :])

        specs = [extra.get(k, SMEM if a.dtype == jnp.int32 else VMEM) for k, a in enumerate(args)]
        out_specs = [pl.BlockSpec(memory_space=pl.ANY) if k in aliases.values() else VMEM for k in range(len(outs))]
        res = call(step, outs, args, [pltpu.VMEM((cols, 3 * w), BF)], specs=specs, out_specs=out_specs, aliases=aliases)
        return res[0], res[1] if more else None, res[-1]

    pair_y = [None] * levels
    acc, message, before = x, y0, None
    before, message, fetched = forward_step(0, swap(0, message), before, acc)
    other = lax.ppermute(fetched, "rhs", [(r, r ^ 1) for r in range(peers)])
    far = [None] + [
        jnp.where(core == l % 2, fetched[(l - 1) // 2], other[(l - 1) // 2]) for l in range(1, levels)
    ]
    for l in range(1, levels):
        before, message, acc = forward_step(l, swap(l, message), before, acc)
        pair_y[l] = before

    def backward_step(l, got, older, above):
        top, more = l == levels - 1, l >= 2
        args = (parity, pair_y[l], B[l - 1], far[l], diag_inv)
        if not top:
            args += (got, older)
        if more:
            args += (S[l - 2], *above)
        n_in = len(args)
        outs = [((cols, 3 * w if more else 2 * w), BF), ((cols, w), BF)]
        if more:
            outs.append(((cols, 3 * w), F32))

        def step(*refs):
            par_ref, y_ref, near_ref, far_ref, d_ref = refs[:5]
            m_ref, z_ref = refs[n_in : n_in + 2]
            e_ref = refs[-1]
            s = side_of(par_ref, l)
            e = y_ref[...]
            if not top:
                g_ref, old_ref = refs[5:7]
                e = e.astype(F32) - g_ref[0, :, : 2 * w].astype(F32) - g_ref[1, :, : 2 * w].astype(F32)
            e_ref[...] = e.astype(BF)
            e_own, e_par = e_ref[:, at(s * w, w)], e_ref[:, at((1 - s) * w, w)]
            z_own = diag_bwd(d_ref, l, e_own)
            z_ref[...] = z_own
            part = dot_n(e_own, near_ref[:, at(s * w, 2 * w)])
            extra = dot_n(e_par, far_ref[...])
            if not top:
                part = part + old_ref[:, at(s * w, 2 * w)]
                extra = extra + g_ref[1 - s, :, 2 * w :].astype(F32)
            for k in range(2):
                half = part[:, k * w : (k + 1) * w]
                m_ref[:, k * w : (k + 1) * w] = jnp.where(s == 1 - k, half + extra, half).astype(BF)
            if more:
                s_ref, old_out = refs[n_in - 1 - len(above)], refs[n_in + 2]
                sums = dot_n(z_own, s_ref[w : 2 * w, :])
                for k, zr in enumerate(refs[n_in - len(above) : n_in]):
                    sums = sums + dot_n(zr[...], s_ref[(k + 2) * w : (k + 3) * w, :])
                old_out[...] = sums
                m_ref[:, 2 * w :] = old_out[:, at(s * 2 * w, w)].astype(BF)

        res = call(step, outs, args, [pltpu.VMEM((cols, 2 * w), BF)])
        return res[0], res[1], res[2] if more else None

    z = [None] * levels
    got, older = None, None
    for l in range(levels - 1, 0, -1):
        message, z[l], older = backward_step(l, got, older, z[l + 1 :])
        got = swap(l - 1, message)

    def finish(par_ref, g_ref, y_ref, d_ref, *rest):
        o_ref = rest[-1]
        here = at(par_ref[0] * w, w)
        terms = g_ref[0, :, here].astype(F32) + g_ref[1, :, here].astype(F32)
        e = (y_ref[...].astype(F32) - terms).astype(BF)
        values = [diag_bwd(d_ref, 0, e).astype(F32)] + [r[...].astype(F32) for r in rest[:-1]]
        for j in range(peers):
            parts = [v[:, j * piece : (j + 1) * piece] for v in values]
            o_ref[j] = jnp.concatenate(parts, axis=1).astype(BF)

    (result,) = call(finish, [((peers, cols, levels * piece), BF)], (parity, got, y0, diag_inv, *z[1:]))
    result = lax.all_to_all(result, "rhs", split_axis=0, concat_axis=0, tiled=True)

    def turn(r_ref, o_ref):
        for j in range(peers):
            o_ref[:, j * cols : (j + 1) * cols] = r_ref[j].astype(F32).T.astype(BF)

    (result,) = call(turn, [((levels * piece, total), BF)], (result,))
    return result.reshape(levels, piece, total).transpose(2, 0, 1)


def solution(mesh):
    placed = (
        P(None, None, ("sn", "rhs")),
        P(None, "sn", None, None),
        P(None, "sn", None, None),
        P(),
        P(),
    )
    return jax.shard_map(
        on_device,
        mesh=mesh,
        in_specs=placed,
        out_specs=P(None, None, ("sn", "rhs")),
        check_vma=False,
    )
```

```python
import jax
import jax.numpy as jnp
from jax import lax
from jax.experimental import pallas as pl
from jax.experimental.pallas import tpu as pltpu
from jax.sharding import PartitionSpec as P

BF = jnp.bfloat16
F32 = jnp.float32
VMEM = pl.BlockSpec(memory_space=pltpu.VMEM)
SMEM = pl.BlockSpec(memory_space=pltpu.SMEM)
HBM = pl.BlockSpec(memory_space=pltpu.HBM)


def dot_t(a, w):
    return lax.dot_general(a, w, (((1,), (1,)), ((), ())), preferred_element_type=F32)


def dot_n(a, w):
    return lax.dot_general(a, w, (((1,), (0,)), ((), ())), preferred_element_type=F32)


def call(body, outs, args, scratch=(), flops=10**7, mib=12, specs=None, out_specs=None, size=None):
    specs = specs or [SMEM if a.dtype == jnp.int32 else VMEM for a in args]
    if size is None:
        size = sum(a.size * a.dtype.itemsize for a in args)
    return pl.pallas_call(
        body,
        out_shape=[jax.ShapeDtypeStruct(s, d) for s, d in outs],
        in_specs=specs,
        out_specs=out_specs or [VMEM] * len(outs),
        scratch_shapes=list(scratch),
        compiler_params=pltpu.CompilerParams(vmem_limit_bytes=mib * 2**20),
        cost_estimate=pl.CostEstimate(flops=flops, bytes_accessed=size, transcendentals=0),
    )(*args)


def build_operators(tiles, diag, row_slot, col_slot, parity, side_of):
    levels, owned, b, _ = diag.shape
    count = tiles.shape[1]
    tall = owned * b
    wide = 3 * tall

    def body(row_ref, col_ref, par_ref, t_ref, d_ref, *refs):
        outs, (scratch, held, sems, in_sems) = refs[: 2 * levels], refs[2 * levels :]
        s_out, b_out, sends = outs[: levels - 1], outs[levels - 1 : 2 * levels - 2], outs[-2:]
        loads = [
            pltpu.make_async_copy(t_ref.at[l], held.at[l], in_sems.at[l]) for l in range(levels - 1)
        ]
        for c in loads:
            c.start()
        copies = []
        for l in range(levels - 1):
            size = (levels - 1 - l) * tall
            start = sum((levels - 1 - k) * tall for k in range(l))
            buf = scratch.at[pl.ds(start, size), :]
            buf[...] = jnp.zeros((size, wide), BF)
            loads[l].wait()

            def add(t, carry):
                r = pl.multiple_of(row_ref[l, t] * b, b)
                c = pl.multiple_of(col_ref[l, t] * b, b)
                at = (pl.ds(r, b), pl.ds(c, b))
                buf[at] = buf[at] + held[l, t]
                return carry

            lax.fori_loop(0, count, add, 0, unroll=8)
            copies.append(pltpu.make_async_copy(buf, s_out[l], sems.at[l]))
            copies[-1].start()
            for q in range(owned):
                rows = slice(q * b, (q + 1) * b)
                b_out[l][rows, :] = dot_n(d_ref[l + 1, q], buf[rows, :]).astype(BF)
            s = side_of(par_ref, l + 1)
            toward = pl.ds(pl.multiple_of((1 - s) * 2 * tall, tall), tall)
            sends[l % 2][l // 2] = b_out[l][:, toward]
        for c in copies:
            c.wait()

    outs = [(((levels - 1 - l) * tall, wide), BF) for l in range(levels - 1)]
    outs += [((tall, wide), BF)] * (levels - 1)
    outs += [((levels // 2, tall, tall), BF), (((levels - 1) // 2, tall, tall), BF)]
    res = call(
        body,
        outs,
        (row_slot, col_slot, parity, tiles, diag),
        [
            pltpu.VMEM((levels * (levels - 1) // 2 * tall, wide), BF),
            pltpu.VMEM(tiles.shape, BF),
            pltpu.SemaphoreType.DMA((levels - 1,)),
            pltpu.SemaphoreType.DMA((levels - 1,)),
        ],
        flops=4 * 10**8,
        mib=60,
        specs=[SMEM, SMEM, SMEM, HBM, VMEM],
        out_specs=[HBM] * (levels - 1) + [VMEM] * (levels + 1),
        size=24 * 2**20,
    )
    return res[: levels - 1], res[levels - 1 : 2 * levels - 2], res[-2:]


def on_device(lanczos_block, diag_inv, factor_tiles, tile_rows, tile_cols):
    levels, owned, b = diag_inv.shape[:3]
    group_tiles = factor_tiles.shape[1]
    n = lax.axis_size("sn")
    peers = lax.axis_size("rhs")
    own = lax.axis_index("sn")
    per_level = owned * n
    w = owned * b
    total, _, piece = lanczos_block.shape
    cols = total // peers
    parity = (own % 2).astype(jnp.int32).reshape(1)

    def side_of(par_ref, l):
        return par_ref[0] if l % 2 == 0 else 1 - par_ref[0]

    def pack(x_ref, o_ref):
        v = x_ref[...].T.astype(BF)
        for j in range(peers):
            o_ref[j] = v[j * cols : (j + 1) * cols]

    flat = lanczos_block.transpose(1, 2, 0).reshape(levels * piece, total)
    (sent,) = call(pack, [((peers, cols, levels * piece), BF)], (flat,))
    arrived = lax.all_to_all(sent, "rhs", split_axis=0, concat_axis=0, tiled=True)

    my_rows = lax.dynamic_slice_in_dim(tile_rows, own * group_tiles, group_tiles, 1)
    my_cols = lax.dynamic_slice_in_dim(tile_cols, own * group_tiles, group_tiles, 1)
    above = jnp.arange(1, levels, dtype=jnp.int32)[:, None]
    group = (jnp.arange(group_tiles, dtype=jnp.int32) // (group_tiles // 3))[None, :]
    row_slot = (my_rows // per_level - above) * owned + my_rows % owned
    col_slot = group * owned + my_cols % owned
    sent, factor_tiles = lax.optimization_barrier((sent, factor_tiles))
    S, B, toward = build_operators(factor_tiles, diag_inv, row_slot, col_slot, parity, side_of)

    pairs = [
        [[i, i + 1] for i in range(0, n, 2)],
        [[i, (i + 1) % n] for i in range(1, n, 2)],
    ]
    swaps = [[(p, q) for p, q in g] + [(q, p) for p, q in g] for g in pairs]
    arrived, toward = lax.optimization_barrier((arrived, list(toward)))
    far_odd, far_even = (lax.ppermute(toward[k], "sn", swaps[1 - k]) for k in range(2))
    far = [None] + [(far_odd if l % 2 else far_even)[(l - 1) // 2] for l in range(1, levels)]

    def swap(l, message):
        return lax.all_gather(message, "sn", axis_index_groups=pairs[l % 2])

    def diag_fwd(d_ref, l, f):
        f = f.astype(BF)
        return jnp.concatenate(
            [dot_t(f[:, q * b : (q + 1) * b], d_ref[l, q]) for q in range(owned)], axis=1
        )

    def diag_bwd(d_ref, l, e):
        return jnp.concatenate(
            [dot_n(e[:, q * b : (q + 1) * b], d_ref[l, q]) for q in range(owned)], axis=1
        ).astype(BF)

    def at(start, size):
        return pl.ds(pl.multiple_of(start, w), size)

    def unpack(a_ref, d_ref, x_ref, y_ref):
        for k in range(levels):
            parts = [a_ref[j].astype(F32)[:, k * piece : (k + 1) * piece] for j in range(peers)]
            x_ref[:, k * w : (k + 1) * w] = jnp.concatenate(parts, axis=1)
        y_ref[...] = diag_fwd(d_ref, 0, x_ref[:, :w]).astype(BF)

    x, y0 = call(unpack, [((cols, levels * w), F32), ((cols, w), BF)], (arrived, diag_inv))

    def forward_step(l, got, before, acc):
        more, rest_levels = l + 1 < levels, levels - l - 2
        base = 2 * w if l == 1 else (w if l == 0 else 0)
        args, outs = (parity, got), [((cols, 2 * w), BF)]
        if l:
            args += (B[l - 1], far[l])
        if more:
            args += (B[l], diag_inv, acc)
            outs.append(((cols, 2 * w), BF))
            if l:
                args += (S[l - 1], before)
                if rest_levels:
                    outs.append(((cols, rest_levels * w), F32))
        n_in = len(args)

        def step(*refs):
            par_ref, g_ref = refs[:2]
            p_ref, y3 = refs[n_in], refs[-1]
            s = side_of(par_ref, l)
            if l:
                near_ref, far_ref = refs[2:4]
                y_own, y_par = g_ref[s, :, w:], g_ref[1 - s, :, w:]
                q_own, q_par = g_ref[s, :, :w].astype(F32), g_ref[1 - s, :, :w].astype(F32)
                new = (q_own - dot_t(y_par, near_ref[:, at((1 - s) * 2 * w, w)])).astype(BF)
                p_ref[:, at(s * w, w)] = new
                p_ref[:, at((1 - s) * w, w)] = (q_par - dot_t(y_own, far_ref[...])).astype(BF)
            else:
                p_ref[:, :w] = g_ref[0]
                p_ref[:, w:] = g_ref[1]
                new = g_ref[s]
            if not more:
                return
            m_ref = refs[n_in + 1]
            m_ref[:, w:] = new
            k = 4 if l else 2
            next_ref, d_ref, acc_ref = refs[k : k + 3]
            f = acc_ref[:, base : base + w]
            if l:
                s_ref, before_ref = refs[k + 3 : k + 5]
                y3[:, at(s * w, 2 * w)] = before_ref[...]
                y3[:, at((1 - s) * 2 * w, w)] = y_par
                f = f - dot_t(y3[...], s_ref[w : 2 * w, :])
            h = diag_fwd(d_ref, l + 1, f)
            q = h - dot_t(p_ref[...], next_ref[:, at((1 - s) * w, 2 * w)])
            m_ref[:, :w] = q.astype(BF)
            if l and rest_levels:
                refs[n_in + 2][...] = acc_ref[:, base + w :] - dot_t(y3[...], s_ref[2 * w :, :])

        res = call(step, outs, args, [pltpu.VMEM((cols, 3 * w), BF)])
        return res[0], res[1] if more else None, res[-1] if l else acc

    pair_y = [None] * levels
    acc, message, before = x, y0, None
    for l in range(levels):
        before, message, acc = forward_step(l, swap(l, message), before, acc)
        pair_y[l] = before

    def backward_step(l, got, cot, older, above):
        top, more = l == levels - 1, l >= 2
        args = (parity, pair_y[l - 1], B[l - 1], far[l], diag_inv)
        args += (pair_y[l],) if top else (got, cot, older)
        if more:
            args += (B[l - 2], S[l - 2], *above)
        n_in = len(args)
        outs = [((cols, 2 * w if more else w), BF), ((cols, w), BF), ((cols, w), F32)]
        if more:
            outs.append(((cols, 3 * w), F32))

        def step(*refs):
            par_ref, y_ref, near_ref, far_ref, d_ref = refs[:5]
            m_ref, z_ref, cot_ref = refs[n_in : n_in + 3]
            s = side_of(par_ref, l)
            if top:
                q = refs[5][:, at(s * w, w)]
                down = -dot_n(refs[5][:, at((1 - s) * w, w)], far_ref[...])
            else:
                g_ref, own_ref, old_ref = refs[5:8]
                q = (own_ref[...] + g_ref[1 - s, :, :w].astype(F32)).astype(BF)
                down = g_ref[1 - s, :, w:].astype(F32) - dot_n(g_ref[s, :, :w], far_ref[...])
            z_own = diag_bwd(d_ref, l, q)
            z_ref[...] = z_own
            pair = -dot_n(q, near_ref[:, at(s * w, 2 * w)])
            if not top:
                pair = pair - old_ref[:, at(s * w, 2 * w)]
            left, right = pair[:, :w], pair[:, w:]
            mine = jnp.where(s == 1, left, right) + down + y_ref[:, at((1 - s) * w, w)].astype(F32)
            cot_ref[...] = mine
            m_ref[:, :w] = jnp.where(s == 1, right, left).astype(BF)
            if more:
                k = 6 if top else 8
                next_ref, s_ref, zs, old_out = refs[k], refs[k + 1], refs[k + 2 : n_in], refs[n_in + 3]
                sums = dot_n(z_own, s_ref[w : 2 * w, :])
                for i, zr in enumerate(zs):
                    sums = sums + dot_n(zr[...], s_ref[(i + 2) * w : (i + 3) * w, :])
                old_out[...] = sums
                toward = at(s * 2 * w, w)
                m_ref[:, w:] = (-dot_n(mine.astype(BF), next_ref[:, toward]) - old_out[:, toward]).astype(BF)

        res = call(step, outs, args)
        return res[0], res[1], res[2], res[3] if more else None

    z = [None] * levels
    got, cot, older = None, None, None
    for l in range(levels - 1, 0, -1):
        message, z[l], cot, older = backward_step(l, got, cot, older, z[l + 1 :])
        got = swap(l - 1, message)

    def finish(par_ref, g_ref, y_ref, d_ref, *rest):
        o_ref = rest[-1]
        e = (y_ref[...] + g_ref[1 - par_ref[0]].astype(F32)).astype(BF)
        values = [diag_bwd(d_ref, 0, e).astype(F32)] + [r[...].astype(F32) for r in rest[:-1]]
        for j in range(peers):
            parts = [v[:, j * piece : (j + 1) * piece] for v in values]
            o_ref[j] = jnp.concatenate(parts, axis=1).astype(BF)

    (result,) = call(finish, [((peers, cols, levels * piece), BF)], (parity, got, cot, diag_inv, *z[1:]))
    result = lax.all_to_all(result, "rhs", split_axis=0, concat_axis=0, tiled=True)

    def turn(r_ref, o_ref):
        for j in range(peers):
            o_ref[:, j * cols : (j + 1) * cols] = r_ref[j].astype(F32).T.astype(BF)

    (result,) = call(turn, [((levels * piece, total), BF)], (result,))
    return result.reshape(levels, piece, total).transpose(2, 0, 1)


def solution(mesh):
    placed = (
        P(None, None, ("sn", "rhs")),
        P(None, "sn", None, None),
        P(None, "sn", None, None),
        P(),
        P(),
    )
    return jax.shard_map(
        on_device,
        mesh=mesh,
        in_specs=placed,
        out_specs=P(None, None, ("sn", "rhs")),
        check_vma=False,
    )
```

```python
import jax
import jax.numpy as jnp
from jax import lax
from jax.experimental import pallas as pl
from jax.experimental.pallas import tpu as pltpu
from jax.sharding import PartitionSpec as P

BF = jnp.bfloat16
F32 = jnp.float32
VMEM = pl.BlockSpec(memory_space=pltpu.VMEM)
SMEM = pl.BlockSpec(memory_space=pltpu.SMEM)
HBM = pl.BlockSpec(memory_space=pltpu.HBM)


def dot_t(a, w):
    return lax.dot_general(a, w, (((1,), (1,)), ((), ())), preferred_element_type=F32)


def dot_n(a, w):
    return lax.dot_general(a, w, (((1,), (0,)), ((), ())), preferred_element_type=F32)


def call(body, outs, args, scratch=(), flops=10**7, mib=12, specs=None, out_specs=None, size=None, aliases=None):
    specs = specs or [SMEM if a.dtype == jnp.int32 else VMEM for a in args]
    if size is None:
        size = sum(a.size * a.dtype.itemsize for a in args)
    return pl.pallas_call(
        body,
        out_shape=[jax.ShapeDtypeStruct(s, d) for s, d in outs],
        in_specs=specs,
        out_specs=out_specs or [VMEM] * len(outs),
        scratch_shapes=list(scratch),
        input_output_aliases=aliases or {},
        compiler_params=pltpu.CompilerParams(vmem_limit_bytes=mib * 2**20),
        cost_estimate=pl.CostEstimate(flops=flops, bytes_accessed=size, transcendentals=0),
    )(*args)


def build_operators(tiles, diag, row_slot, col_slot, parity, side_of):
    levels, owned, b, _ = diag.shape
    count = tiles.shape[1]
    tall = owned * b
    wide = 3 * tall

    def body(row_ref, col_ref, par_ref, t_ref, d_ref, *refs):
        outs, (scratch, held, sems, in_sems) = refs[: 2 * levels + 1], refs[2 * levels + 1 :]
        s_out, b_out, sends = outs[: levels - 1], outs[levels - 1 : 2 * levels - 2], outs[-3:]
        loads = [
            pltpu.make_async_copy(t_ref.at[l], held.at[l], in_sems.at[l]) for l in range(levels - 1)
        ]
        for c in loads:
            c.start()
        copies = []
        for l in range(levels - 1):
            size = (levels - 1 - l) * tall
            start = sum((levels - 1 - k) * tall for k in range(l))
            buf = scratch.at[pl.ds(start, size), :]
            buf[...] = jnp.zeros((size, wide), BF)
            loads[l].wait()

            def add(t, carry):
                r = pl.multiple_of(row_ref[l, t] * b, b)
                c = pl.multiple_of(col_ref[l, t] * b, b)
                at = (pl.ds(r, b), pl.ds(c, b))
                buf[at] = buf[at] + held[l, t]
                return carry

            lax.fori_loop(0, count, add, 0, unroll=8)
            copies.append(pltpu.make_async_copy(buf, s_out[l], sems.at[l]))
            copies[-1].start()
            for q in range(owned):
                rows = slice(q * b, (q + 1) * b)
                b_out[l][rows, :] = dot_n(d_ref[l + 1, q], buf[rows, :]).astype(BF)
            s = side_of(par_ref, l + 1)
            toward = pl.ds(pl.multiple_of((1 - s) * 2 * tall, tall), tall)
            sends[0 if l == 0 else 1 + l % 2][(l - 1) // 2 if l else 0] = b_out[l][:, toward]
        for c in copies:
            c.wait()

    outs = [(((levels - 1 - l) * tall, wide), BF) for l in range(levels - 1)]
    outs += [((tall, wide), BF)] * (levels - 1)
    outs += [((k, tall, tall), BF) for k in (1, levels // 2 - 1, (levels - 1) // 2)]
    res = call(
        body,
        outs,
        (row_slot, col_slot, parity, tiles, diag),
        [
            pltpu.VMEM((levels * (levels - 1) // 2 * tall, wide), BF),
            pltpu.VMEM(tiles.shape, BF),
            pltpu.SemaphoreType.DMA((levels - 1,)),
            pltpu.SemaphoreType.DMA((levels - 1,)),
        ],
        flops=4 * 10**8,
        mib=60,
        specs=[SMEM, SMEM, SMEM, HBM, VMEM],
        out_specs=[HBM] * (levels - 1) + [VMEM] * (levels + 2),
        size=24 * 2**20,
    )
    return res[: levels - 1], res[levels - 1 : 2 * levels - 2], res[-3:]


def on_device(lanczos_block, diag_inv, factor_tiles, tile_rows, tile_cols):
    levels, owned, b = diag_inv.shape[:3]
    group_tiles = factor_tiles.shape[1]
    n = lax.axis_size("sn")
    peers = lax.axis_size("rhs")
    own = lax.axis_index("sn")
    per_level = owned * n
    w = owned * b
    total, _, piece = lanczos_block.shape
    cols = total // peers
    parity = (own % 2).astype(jnp.int32).reshape(1)

    def side_of(par_ref, l):
        return par_ref[0] if l % 2 == 0 else 1 - par_ref[0]

    def pack(x_ref, o_ref):
        v = x_ref[...].T.astype(BF)
        for j in range(peers):
            o_ref[j] = v[j * cols : (j + 1) * cols]

    flat = lanczos_block.transpose(1, 2, 0).reshape(levels * piece, total)
    (sent,) = call(pack, [((peers, cols, levels * piece), BF)], (flat,))
    arrived = lax.all_to_all(sent, "rhs", split_axis=0, concat_axis=0, tiled=True)

    my_rows = lax.dynamic_slice_in_dim(tile_rows, own * group_tiles, group_tiles, 1)
    my_cols = lax.dynamic_slice_in_dim(tile_cols, own * group_tiles, group_tiles, 1)
    above = jnp.arange(1, levels, dtype=jnp.int32)[:, None]
    group = (jnp.arange(group_tiles, dtype=jnp.int32) // (group_tiles // 3))[None, :]
    row_slot = (my_rows // per_level - above) * owned + my_rows % owned
    col_slot = group * owned + my_cols % owned
    sent, factor_tiles = lax.optimization_barrier((sent, factor_tiles))
    S, B, toward = build_operators(factor_tiles, diag_inv, row_slot, col_slot, parity, side_of)

    pairs = [
        [[i, i + 1] for i in range(0, n, 2)],
        [[i, (i + 1) % n] for i in range(1, n, 2)],
    ]
    swaps = [[(p, q) for p, q in g] + [(q, p) for p, q in g] for g in pairs]
    arrived, toward = lax.optimization_barrier((arrived, list(toward)))
    far = [None] * levels
    first_far = lax.ppermute(toward[0], "sn", swaps[1])
    far[1] = first_far[0]

    def swap(l, message):
        return lax.all_gather(message, "sn", axis_index_groups=pairs[l % 2])

    def diag_fwd(d_ref, l, f):
        f = f.astype(BF)
        return jnp.concatenate(
            [dot_t(f[:, q * b : (q + 1) * b], d_ref[l, q]) for q in range(owned)], axis=1
        )

    def diag_bwd(d_ref, l, e):
        return jnp.concatenate(
            [dot_n(e[:, q * b : (q + 1) * b], d_ref[l, q]) for q in range(owned)], axis=1
        ).astype(BF)

    def at(start, size):
        return pl.ds(pl.multiple_of(start, w), size)

    def unpack(a_ref, d_ref, x_ref, y_ref):
        for k in range(levels):
            parts = [a_ref[j].astype(F32)[:, k * piece : (k + 1) * piece] for j in range(peers)]
            x_ref[:, k * w : (k + 1) * w] = jnp.concatenate(parts, axis=1)
        y_ref[...] = diag_fwd(d_ref, 0, x_ref[:, :w]).astype(BF)

    x, y0 = call(unpack, [((cols, levels * w), F32), ((cols, w), BF)], (arrived, diag_inv))

    def forward_step(l, got, before, acc):
        more, rest_levels = l + 1 < levels, levels - l - 2
        base = 2 * w if l == 1 else (w if l == 0 else 0)
        args, outs = (parity, got), [((cols, 2 * w), BF)]
        if l:
            args += (B[l - 1], far[l])
        if more:
            args += (B[l], diag_inv, acc)
            outs.append(((cols, 2 * w), BF))
            if l:
                args += (S[l - 1], before)
                if rest_levels:
                    outs.append(((cols, rest_levels * w), F32))
        aliases, extra = {}, {}
        if l < 2:
            carried = toward[2 - l]
            aliases, extra = {len(args): len(outs)}, {len(args): pl.BlockSpec(memory_space=pl.ANY)}
            args += (carried,)
            outs.append((carried.shape, BF))
        if l == 0:
            extra[len(args)] = pl.BlockSpec(memory_space=pl.ANY)
            args += (first_far,)
        n_in = len(args)

        def step(*refs):
            par_ref, g_ref = refs[:2]
            p_ref, y3 = refs[n_in], refs[-1]
            s = side_of(par_ref, l)
            if l:
                near_ref, far_ref = refs[2:4]
                y_own, y_par = g_ref[s, :, w:], g_ref[1 - s, :, w:]
                q_own, q_par = g_ref[s, :, :w].astype(F32), g_ref[1 - s, :, :w].astype(F32)
                new = (q_own - dot_t(y_par, near_ref[:, at((1 - s) * 2 * w, w)])).astype(BF)
                p_ref[:, at(s * w, w)] = new
                p_ref[:, at((1 - s) * w, w)] = (q_par - dot_t(y_own, far_ref[...])).astype(BF)
            else:
                p_ref[:, :w] = g_ref[0]
                p_ref[:, w:] = g_ref[1]
                new = g_ref[s]
            if not more:
                return
            m_ref = refs[n_in + 1]
            m_ref[:, w:] = new
            k = 4 if l else 2
            next_ref, d_ref, acc_ref = refs[k : k + 3]
            f = acc_ref[:, base : base + w]
            if l:
                s_ref, before_ref = refs[k + 3 : k + 5]
                y3[:, at(s * w, 2 * w)] = before_ref[...]
                y3[:, at((1 - s) * 2 * w, w)] = y_par
                f = f - dot_t(y3[...], s_ref[w : 2 * w, :])
            h = diag_fwd(d_ref, l + 1, f)
            q = h - dot_t(p_ref[...], next_ref[:, at((1 - s) * w, 2 * w)])
            m_ref[:, :w] = q.astype(BF)
            if l and rest_levels:
                refs[n_in + 2][...] = acc_ref[:, base + w :] - dot_t(y3[...], s_ref[2 * w :, :])

        specs = [extra.get(k, SMEM if a.dtype == jnp.int32 else VMEM) for k, a in enumerate(args)]
        out_specs = [pl.BlockSpec(memory_space=pl.ANY) if k in aliases.values() else VMEM for k in range(len(outs))]
        res = list(call(step, outs, args, [pltpu.VMEM((cols, 3 * w), BF)], specs=specs, out_specs=out_specs, aliases=aliases))
        passed = res.pop() if l < 2 else None
        return res[0], res[1] if more else None, res[-1], passed

    pair_y = [None] * levels
    pair_y[0], message, _, carried = forward_step(0, swap(0, y0), None, x)
    acc = x
    for l in range(1, levels):
        if l < 3:
            fetched = lax.ppermute(carried, "sn", swaps[l - 1])
            for k in range(l + 1, levels, 2):
                far[k] = fetched[(k - l - 1) // 2]
        got = swap(l, message)
        pair_y[l], message, acc, carried = forward_step(l, got, pair_y[l - 1], acc)

    def backward_step(l, got, cot, older, above):
        top, more = l == levels - 1, l >= 2
        args = (parity, pair_y[l - 1], B[l - 1], far[l], diag_inv)
        args += (pair_y[l],) if top else (got, cot, older)
        if more:
            args += (B[l - 2], S[l - 2], *above)
        n_in = len(args)
        outs = [((cols, 2 * w if more else w), BF), ((cols, w), BF), ((cols, w), F32)]
        if more:
            outs.append(((cols, 3 * w), F32))

        def step(*refs):
            par_ref, y_ref, near_ref, far_ref, d_ref = refs[:5]
            m_ref, z_ref, cot_ref = refs[n_in : n_in + 3]
            s = side_of(par_ref, l)
            if top:
                q = refs[5][:, at(s * w, w)]
                down = -dot_n(refs[5][:, at((1 - s) * w, w)], far_ref[...])
            else:
                g_ref, own_ref, old_ref = refs[5:8]
                q = (own_ref[...] + g_ref[1 - s, :, :w].astype(F32)).astype(BF)
                down = g_ref[1 - s, :, w:].astype(F32) - dot_n(g_ref[s, :, :w], far_ref[...])
            z_own = diag_bwd(d_ref, l, q)
            z_ref[...] = z_own
            pair = -dot_n(q, near_ref[:, at(s * w, 2 * w)])
            if not top:
                pair = pair - old_ref[:, at(s * w, 2 * w)]
            left, right = pair[:, :w], pair[:, w:]
            mine = jnp.where(s == 1, left, right) + down + y_ref[:, at((1 - s) * w, w)].astype(F32)
            cot_ref[...] = mine
            m_ref[:, :w] = jnp.where(s == 1, right, left).astype(BF)
            if more:
                k = 6 if top else 8
                next_ref, s_ref, zs, old_out = refs[k], refs[k + 1], refs[k + 2 : n_in], refs[n_in + 3]
                sums = dot_n(z_own, s_ref[w : 2 * w, :])
                for i, zr in enumerate(zs):
                    sums = sums + dot_n(zr[...], s_ref[(i + 2) * w : (i + 3) * w, :])
                old_out[...] = sums
                toward = at(s * 2 * w, w)
                m_ref[:, w:] = (-dot_n(mine.astype(BF), next_ref[:, toward]) - old_out[:, toward]).astype(BF)

        res = call(step, outs, args)
        return res[0], res[1], res[2], res[3] if more else None

    z = [None] * levels
    got, cot, older = None, None, None
    for l in range(levels - 1, 0, -1):
        message, z[l], cot, older = backward_step(l, got, cot, older, z[l + 1 :])
        got = swap(l - 1, message)

    def finish(par_ref, g_ref, y_ref, d_ref, *rest):
        o_ref = rest[-1]
        e = (y_ref[...] + g_ref[1 - par_ref[0]].astype(F32)).astype(BF)
        values = [diag_bwd(d_ref, 0, e).astype(F32)] + [r[...].astype(F32) for r in rest[:-1]]
        for j in range(peers):
            parts = [v[:, j * piece : (j + 1) * piece] for v in values]
            o_ref[j] = jnp.concatenate(parts, axis=1).astype(BF)

    (result,) = call(finish, [((peers, cols, levels * piece), BF)], (parity, got, cot, diag_inv, *z[1:]))
    result = lax.all_to_all(result, "rhs", split_axis=0, concat_axis=0, tiled=True)

    def turn(r_ref, o_ref):
        for j in range(peers):
            o_ref[:, j * cols : (j + 1) * cols] = r_ref[j].astype(F32).T.astype(BF)

    (result,) = call(turn, [((levels * piece, total), BF)], (result,))
    return result.reshape(levels, piece, total).transpose(2, 0, 1)


def solution(mesh):
    placed = (
        P(None, None, ("sn", "rhs")),
        P(None, "sn", None, None),
        P(None, "sn", None, None),
        P(),
        P(),
    )
    return jax.shard_map(
        on_device,
        mesh=mesh,
        in_specs=placed,
        out_specs=P(None, None, ("sn", "rhs")),
        check_vma=False,
    )
```

```python
import jax
import jax.numpy as jnp
from jax import lax
from jax.experimental import pallas as pl
from jax.experimental.pallas import tpu as pltpu
from jax.sharding import PartitionSpec as P

BF = jnp.bfloat16
F32 = jnp.float32
VMEM = pl.BlockSpec(memory_space=pltpu.VMEM)
SMEM = pl.BlockSpec(memory_space=pltpu.SMEM)
HBM = pl.BlockSpec(memory_space=pltpu.HBM)


def dot_t(a, w):
    return lax.dot_general(a, w, (((1,), (1,)), ((), ())), preferred_element_type=F32)


def dot_n(a, w):
    return lax.dot_general(a, w, (((1,), (0,)), ((), ())), preferred_element_type=F32)


def call(body, outs, args, scratch=(), flops=10**7, mib=12, specs=None, out_specs=None, size=None):
    specs = specs or [SMEM if a.dtype == jnp.int32 else VMEM for a in args]
    if size is None:
        size = sum(a.size * a.dtype.itemsize for a in args)
    return pl.pallas_call(
        body,
        out_shape=[jax.ShapeDtypeStruct(s, d) for s, d in outs],
        in_specs=specs,
        out_specs=out_specs or [VMEM] * len(outs),
        scratch_shapes=list(scratch),
        compiler_params=pltpu.CompilerParams(vmem_limit_bytes=mib * 2**20),
        cost_estimate=pl.CostEstimate(flops=flops, bytes_accessed=size, transcendentals=0),
    )(*args)


def build_operators(tiles, diag, row_slot, col_slot, parity, side_of):
    levels, owned, b, _ = diag.shape
    count = tiles.shape[1]
    tall = owned * b
    wide = 3 * tall

    def body(row_ref, col_ref, par_ref, t_ref, d_ref, *refs):
        outs, (scratch, held, sems, in_sems) = refs[: 2 * levels], refs[2 * levels :]
        s_out, b_out, sends = outs[: levels - 1], outs[levels - 1 : 2 * levels - 2], outs[-2:]
        loads = [
            pltpu.make_async_copy(t_ref.at[l], held.at[l], in_sems.at[l]) for l in range(levels - 1)
        ]
        for c in loads:
            c.start()
        copies = []
        for l in range(levels - 1):
            size = (levels - 1 - l) * tall
            start = sum((levels - 1 - k) * tall for k in range(l))
            buf = scratch.at[pl.ds(start, size), :]
            buf[...] = jnp.zeros((size, wide), BF)
            loads[l].wait()

            def add(t, carry):
                r = pl.multiple_of(row_ref[l, t] * b, b)
                c = pl.multiple_of(col_ref[l, t] * b, b)
                at = (pl.ds(r, b), pl.ds(c, b))
                buf[at] = buf[at] + held[l, t]
                return carry

            lax.fori_loop(0, count, add, 0, unroll=24)
            copies.append(pltpu.make_async_copy(buf, s_out[l], sems.at[l]))
            copies[-1].start()
            for q in range(owned):
                rows = slice(q * b, (q + 1) * b)
                b_out[l][rows, :] = dot_n(d_ref[l + 1, q], buf[rows, :]).astype(BF)
            s = side_of(par_ref, l + 1)
            toward = pl.ds(pl.multiple_of((1 - s) * 2 * tall, tall), tall)
            sends[l % 2][l // 2] = b_out[l][:, toward]
        for c in copies:
            c.wait()

    outs = [(((levels - 1 - l) * tall, wide), BF) for l in range(levels - 1)]
    outs += [((tall, wide), BF)] * (levels - 1)
    outs += [((levels // 2, tall, tall), BF), (((levels - 1) // 2, tall, tall), BF)]
    res = call(
        body,
        outs,
        (row_slot, col_slot, parity, tiles, diag),
        [
            pltpu.VMEM((levels * (levels - 1) // 2 * tall, wide), BF),
            pltpu.VMEM(tiles.shape, BF),
            pltpu.SemaphoreType.DMA((levels - 1,)),
            pltpu.SemaphoreType.DMA((levels - 1,)),
        ],
        flops=4 * 10**8,
        mib=60,
        specs=[SMEM, SMEM, SMEM, HBM, VMEM],
        out_specs=[HBM] * (levels - 1) + [VMEM] * (levels + 1),
        size=24 * 2**20,
    )
    return res[: levels - 1], res[levels - 1 : 2 * levels - 2], res[-2:]


def on_device(lanczos_block, diag_inv, factor_tiles, tile_rows, tile_cols):
    levels, owned, b = diag_inv.shape[:3]
    group_tiles = factor_tiles.shape[1]
    n = lax.axis_size("sn")
    peers = lax.axis_size("rhs")
    own = lax.axis_index("sn")
    per_level = owned * n
    w = owned * b
    total, _, piece = lanczos_block.shape
    cols = total // peers
    parity = (own % 2).astype(jnp.int32).reshape(1)

    def side_of(par_ref, l):
        return par_ref[0] if l % 2 == 0 else 1 - par_ref[0]

    def pack(x_ref, o_ref):
        v = x_ref[...].T.astype(BF)
        for j in range(peers):
            o_ref[j] = v[j * cols : (j + 1) * cols]

    flat = lanczos_block.transpose(1, 2, 0).reshape(levels * piece, total)
    (sent,) = call(pack, [((peers, cols, levels * piece), BF)], (flat,))
    arrived = lax.all_to_all(sent, "rhs", split_axis=0, concat_axis=0, tiled=True)

    my_rows = lax.dynamic_slice_in_dim(tile_rows, own * group_tiles, group_tiles, 1)
    my_cols = lax.dynamic_slice_in_dim(tile_cols, own * group_tiles, group_tiles, 1)
    above = jnp.arange(1, levels, dtype=jnp.int32)[:, None]
    group = (jnp.arange(group_tiles, dtype=jnp.int32) // (group_tiles // 3))[None, :]
    row_slot = (my_rows // per_level - above) * owned + my_rows % owned
    col_slot = group * owned + my_cols % owned
    sent, factor_tiles = lax.optimization_barrier((sent, factor_tiles))
    S, B, toward = build_operators(factor_tiles, diag_inv, row_slot, col_slot, parity, side_of)

    pairs = [
        [[i, i + 1] for i in range(0, n, 2)],
        [[i, (i + 1) % n] for i in range(1, n, 2)],
    ]
    swaps = [[(p, q) for p, q in g] + [(q, p) for p, q in g] for g in pairs]
    arrived, toward = lax.optimization_barrier((arrived, list(toward)))
    far_odd, far_even = (lax.ppermute(toward[k], "sn", swaps[1 - k]) for k in range(2))
    far = [None] + [(far_odd if l % 2 else far_even)[(l - 1) // 2] for l in range(1, levels)]

    def swap(l, message):
        return lax.all_gather(message, "sn", axis_index_groups=pairs[l % 2])

    def diag_fwd(d_ref, l, f):
        f = f.astype(BF)
        return jnp.concatenate(
            [dot_t(f[:, q * b : (q + 1) * b], d_ref[l, q]) for q in range(owned)], axis=1
        )

    def diag_bwd(d_ref, l, e):
        return jnp.concatenate(
            [dot_n(e[:, q * b : (q + 1) * b], d_ref[l, q]) for q in range(owned)], axis=1
        ).astype(BF)

    def at(start, size):
        return pl.ds(pl.multiple_of(start, w), size)

    def unpack(a_ref, d_ref, x_ref, y_ref):
        for k in range(levels):
            parts = [a_ref[j].astype(F32)[:, k * piece : (k + 1) * piece] for j in range(peers)]
            x_ref[:, k * w : (k + 1) * w] = jnp.concatenate(parts, axis=1)
        y_ref[...] = diag_fwd(d_ref, 0, x_ref[:, :w]).astype(BF)

    x, y0 = call(unpack, [((cols, levels * w), F32), ((cols, w), BF)], (arrived, diag_inv))

    def forward_step(l, got, before, acc):
        more, rest_levels = l + 1 < levels, levels - l - 2
        base = 2 * w if l == 1 else (w if l == 0 else 0)
        args, outs = (parity, got), [((cols, 2 * w), BF)]
        if l:
            args += (B[l - 1], far[l])
        if more:
            args += (B[l], diag_inv, acc)
            outs.append(((cols, 2 * w), BF))
            if l:
                args += (S[l - 1], before)
                if rest_levels:
                    outs.append(((cols, rest_levels * w), F32))
        n_in = len(args)

        def step(*refs):
            par_ref, g_ref = refs[:2]
            p_ref, y3 = refs[n_in], refs[-1]
            s = side_of(par_ref, l)
            if l:
                near_ref, far_ref = refs[2:4]
                y_own, y_par = g_ref[s, :, w:], g_ref[1 - s, :, w:]
                q_own, q_par = g_ref[s, :, :w].astype(F32), g_ref[1 - s, :, :w].astype(F32)
                new = (q_own - dot_t(y_par, near_ref[:, at((1 - s) * 2 * w, w)])).astype(BF)
                p_ref[:, at(s * w, w)] = new
                p_ref[:, at((1 - s) * w, w)] = (q_par - dot_t(y_own, far_ref[...])).astype(BF)
            else:
                p_ref[:, :w] = g_ref[0]
                p_ref[:, w:] = g_ref[1]
                new = g_ref[s]
            if not more:
                return
            m_ref = refs[n_in + 1]
            m_ref[:, w:] = new
            k = 4 if l else 2
            next_ref, d_ref, acc_ref = refs[k : k + 3]
            f = acc_ref[:, base : base + w]
            if l:
                s_ref, before_ref = refs[k + 3 : k + 5]
                y3[:, at(s * w, 2 * w)] = before_ref[...]
                y3[:, at((1 - s) * 2 * w, w)] = y_par
                f = f - dot_t(y3[...], s_ref[w : 2 * w, :])
            h = diag_fwd(d_ref, l + 1, f)
            q = h - dot_t(p_ref[...], next_ref[:, at((1 - s) * w, 2 * w)])
            m_ref[:, :w] = q.astype(BF)
            if l and rest_levels:
                refs[n_in + 2][...] = acc_ref[:, base + w :] - dot_t(y3[...], s_ref[2 * w :, :])

        res = call(step, outs, args, [pltpu.VMEM((cols, 3 * w), BF)])
        return res[0], res[1] if more else None, res[-1] if l else acc

    pair_y = [None] * levels
    acc, message, before = x, y0, None
    for l in range(levels):
        before, message, acc = forward_step(l, swap(l, message), before, acc)
        pair_y[l] = before

    def backward_step(l, got, cot, older, above):
        top, more = l == levels - 1, l >= 2
        args = (parity, pair_y[l - 1], B[l - 1], far[l], diag_inv)
        args += (pair_y[l],) if top else (got, cot, older)
        if more:
            args += (B[l - 2], S[l - 2], *above)
        n_in = len(args)
        outs = [((cols, 2 * w if more else w), BF), ((cols, w), BF), ((cols, w), F32)]
        if more:
            outs.append(((cols, 3 * w), F32))

        def step(*refs):
            par_ref, y_ref, near_ref, far_ref, d_ref = refs[:5]
            m_ref, z_ref, cot_ref = refs[n_in : n_in + 3]
            s = side_of(par_ref, l)
            if top:
                q = refs[5][:, at(s * w, w)]
                down = -dot_n(refs[5][:, at((1 - s) * w, w)], far_ref[...])
            else:
                g_ref, own_ref, old_ref = refs[5:8]
                q = (own_ref[...] + g_ref[1 - s, :, :w].astype(F32)).astype(BF)
                down = g_ref[1 - s, :, w:].astype(F32) - dot_n(g_ref[s, :, :w], far_ref[...])
            z_own = diag_bwd(d_ref, l, q)
            z_ref[...] = z_own
            pair = -dot_n(q, near_ref[:, at(s * w, 2 * w)])
            if not top:
                pair = pair - old_ref[:, at(s * w, 2 * w)]
            left, right = pair[:, :w], pair[:, w:]
            mine = jnp.where(s == 1, left, right) + down + y_ref[:, at((1 - s) * w, w)].astype(F32)
            cot_ref[...] = mine
            m_ref[:, :w] = jnp.where(s == 1, right, left).astype(BF)
            if more:
                k = 6 if top else 8
                next_ref, s_ref, zs, old_out = refs[k], refs[k + 1], refs[k + 2 : n_in], refs[n_in + 3]
                sums = dot_n(z_own, s_ref[w : 2 * w, :])
                for i, zr in enumerate(zs):
                    sums = sums + dot_n(zr[...], s_ref[(i + 2) * w : (i + 3) * w, :])
                old_out[...] = sums
                toward = at(s * 2 * w, w)
                m_ref[:, w:] = (-dot_n(mine.astype(BF), next_ref[:, toward]) - old_out[:, toward]).astype(BF)

        res = call(step, outs, args)
        return res[0], res[1], res[2], res[3] if more else None

    z = [None] * levels
    got, cot, older = None, None, None
    for l in range(levels - 1, 0, -1):
        message, z[l], cot, older = backward_step(l, got, cot, older, z[l + 1 :])
        got = swap(l - 1, message)

    def finish(par_ref, g_ref, y_ref, d_ref, *rest):
        o_ref = rest[-1]
        e = (y_ref[...] + g_ref[1 - par_ref[0]].astype(F32)).astype(BF)
        values = [diag_bwd(d_ref, 0, e).astype(F32)] + [r[...].astype(F32) for r in rest[:-1]]
        for j in range(peers):
            parts = [v[:, j * piece : (j + 1) * piece] for v in values]
            o_ref[j] = jnp.concatenate(parts, axis=1).astype(BF)

    (result,) = call(finish, [((peers, cols, levels * piece), BF)], (parity, got, cot, diag_inv, *z[1:]))
    result = lax.all_to_all(result, "rhs", split_axis=0, concat_axis=0, tiled=True)

    def turn(r_ref, o_ref):
        for j in range(peers):
            o_ref[:, j * cols : (j + 1) * cols] = r_ref[j].astype(F32).T.astype(BF)

    (result,) = call(turn, [((levels * piece, total), BF)], (result,))
    return result.reshape(levels, piece, total).transpose(2, 0, 1)


def solution(mesh):
    placed = (
        P(None, None, ("sn", "rhs")),
        P(None, "sn", None, None),
        P(None, "sn", None, None),
        P(),
        P(),
    )
    return jax.shard_map(
        on_device,
        mesh=mesh,
        in_specs=placed,
        out_specs=P(None, None, ("sn", "rhs")),
        check_vma=False,
    )
```
